256 devices in a mesh: lat: 64 (over z, y_lo, x), lon: 4 (over y_hi, core).
Axes of the slice: x: 4, y: 4 (y_hi: 2, y_lo: 2; y = y_hi * 2 + y_lo), z: 8, core: 2. Of those that a mesh axis runs over, the one named last changes fastest.
Arguments:
- field: bfloat16 [256, 768, 256], P('lat', 'lon'), may hold values from -6 to 6
- cotangent: bfloat16 [256, 768, 256], P('lat', 'lon'), may hold values from -6 to 6
- legendre: bfloat16 [16, 384, 256], P(None, None, 'lat'), as said below
- cycle_weight: float32 [256], P('lat'), may hold values from 0.5 to 1.5
- support_tap: int32 [256, 18], replicated, may hold values from 0 to 8
- support_basis: int32 [256, 18], replicated, may hold values from 0 to 3
- support_weight: float32 [256, 18], replicated, may hold values from 0.5 to 2
- filter_weight: bfloat16 [4, 256, 256], replicated, may hold values from -0.1875 to 0.1875
- spectral_weight: bfloat16 [256, 256], replicated, may hold values from -0.375 to 0.375
- spectral_gain: bfloat16 [384, 256], P('lat', 'lon'), may hold values from 0.5 to 2
Outputs:
- output: bfloat16 [256, 768, 256], P('lat', 'lon')
- grad_field: bfloat16 [256, 768, 256], P('lat', 'lon')
- grad_filter: float32 [4, 256, 256], replicated
- grad_spectral: float32 [256, 256], P(None, 'lon')
The draws below stay inside these ranges and needn't reach their ends.
Inputs may be any that keep to these rules, and one draw needn't show every extreme that they name: legendre[t, l, i] is zero wherever l < t, and lies within -4 / sqrt(256) to 4 / sqrt(256).
All inputs are finite; a program needn't handle non-finite values.
Results may differ from the reference program's by a relative error of at most 0.019.
Values may be sent and summed in bfloat16 or wider, within the bound.
A program may use at most 64 MiB of HBM per device.

```python
import math
import jax
import jax.numpy as jnp
from jax import lax

CYCLES = 4
LATITUDES = 256
LONGITUDES = 768
CHANNELS = 256
DEGREES = 384
ORDERS = 16
BASIS_COUNT = 4
SUPPORT = 18


def draw_legendre(key, part):
    key = jax.random.fold_in(key, 11)
    scale = LATITUDES ** (-0.5)
    degree = jnp.arange(DEGREES, dtype=jnp.int32)[None, :, None]
    first = jnp.arange(ORDERS, dtype=jnp.int32)[:, None, None]
    keep = (degree >= first).astype(jnp.float32)
    values = jax.random.truncated_normal(key, -4.0, 4.0, (ORDERS, DEGREES, LATITUDES), jnp.float32)
    return (values * keep * scale).astype(jnp.bfloat16)


def with_ends(entries, key, low, largest):
    longest = entries.shape.index(max(entries.shape))
    spots = []
    for shift in (0, 1):
        where = [jax.random.randint(jax.random.fold_in(key, axis), (), 0, length) for axis, length in enumerate(entries.shape)]
        where[longest] = (where[longest] + shift) % entries.shape[longest]
        spots.append(tuple(where))
    return entries.at[spots[0]].set(low).at[spots[1]].set(largest)


def levels(stream_key, extent, cuts, least, top_value):
    loudness, own = 1.0, jax.random.fold_in(stream_key, 6)
    for position, shards_of in cuts:
        heights = jnp.exp(jax.random.uniform(jax.random.fold_in(own, position), (shards_of,), jnp.float32, least / len(cuts), top_value / len(cuts)))
        loudness = loudness * jnp.repeat(heights, extent[position] // shards_of).reshape([-1 if axis == position else 1 for axis in range(len(extent))])
    return loudness


def centred(own_key, extent, scale, reach, cuts=(), kind=jnp.bfloat16):
    values = scale * jax.random.normal(own_key, extent, jnp.float32)
    if cuts:
        values = values * levels(own_key, extent, cuts, -0.22, 0.18)
    return jnp.clip(values, -reach, reach).astype(kind)


def setup_inputs(seed: int = 0) -> dict:
    arg_keys = jax.random.split(jax.random.key(seed), 11)
    field = centred(arg_keys[0], (LATITUDES, LONGITUDES, CHANNELS), 1.0, 6.0, ((0, 64), (1, 4)))
    cotangent = centred(arg_keys[1], (LATITUDES, LONGITUDES, CHANNELS), 1.0, 6.0, ((0, 64), (1, 4)))
    legendre = draw_legendre(jax.random.fold_in(arg_keys[10], 71), 0)
    cycle_weight = jnp.clip(0.5 + 1.0 * jax.random.uniform(arg_keys[3], (LATITUDES,), jnp.float32) ** levels(arg_keys[3], (LATITUDES,), ((0, 64),), -0.2, 0.2), 0.5, 1.5)
    support_tap = with_ends(jax.random.randint(arg_keys[4], (LATITUDES, SUPPORT), 0, 9), jax.random.fold_in(arg_keys[4], 1), 0, 8).astype(jnp.int32)
    support_basis = with_ends(jax.random.randint(arg_keys[5], (LATITUDES, SUPPORT), 0, BASIS_COUNT), jax.random.fold_in(arg_keys[5], 1), 0, BASIS_COUNT - 1).astype(jnp.int32)
    support_weight = jnp.clip(jnp.exp(jax.random.uniform(arg_keys[6], (LATITUDES, SUPPORT), jnp.float32, math.log(0.5), math.log(2.0))), 0.5, 2.0)
    filter_weight = centred(arg_keys[7], (BASIS_COUNT, CHANNELS, CHANNELS), (BASIS_COUNT * CHANNELS) ** -0.5, 0.1875)
    spectral_weight = centred(arg_keys[8], (CHANNELS, CHANNELS), CHANNELS ** -0.5, 0.375)
    spectral_gain = jnp.clip(jnp.exp(math.log(2.0) - 1.3862944 * jax.random.uniform(arg_keys[9], (DEGREES, CHANNELS), jnp.float32) ** levels(arg_keys[9], (DEGREES, CHANNELS), ((0, 64), (1, 4)), -0.2, 0.2)), 0.5, 2.0).astype(jnp.bfloat16)
    return {"field": field, "cotangent": cotangent, "legendre": legendre, "cycle_weight": cycle_weight, "support_tap": support_tap, "support_basis": support_basis, "support_weight": support_weight, "filter_weight": filter_weight, "spectral_weight": spectral_weight, "spectral_gain": spectral_gain}


def tap_table(support_tap, support_basis, support_weight):
    tap_onehot = (support_tap[:, :, None] == jnp.arange(9, dtype=jnp.int32)[None, None, :]).astype(jnp.float32)
    basis_onehot = (support_basis[:, :, None] == jnp.arange(BASIS_COUNT, dtype=jnp.int32)[None, None, :]).astype(jnp.float32)
    table = jnp.einsum('ist,isk->itk', tap_onehot * support_weight[:, :, None], basis_onehot, precision=lax.Precision.HIGHEST)
    return table.astype(jnp.bfloat16)


def trig_table(scale):
    longitude = jnp.arange(LONGITUDES, dtype=jnp.int32)
    order = jnp.arange(ORDERS, dtype=jnp.int32)
    turns = (longitude[:, None] * order[None, :]) % LONGITUDES
    angle = turns.astype(jnp.float32) * (2.0 * math.pi / LONGITUDES)
    return (jnp.stack([jnp.cos(angle), jnp.sin(angle)], axis=1) * scale).astype(jnp.bfloat16)


def wrap_columns(values):
    return jnp.concatenate([values[:, -1:], values, values[:, :1]], axis=1)


def filter_rows(extended, tap_rows):
    count = extended.shape[0] - 2
    width = extended.shape[1] - 2
    shifted = jnp.stack([extended[north:north + count, east:east + width] for north in range(3) for east in range(3)], axis=1)
    summed = jnp.einsum('atk,atjc->akjc', tap_rows.astype(jnp.float32), shifted.astype(jnp.float32))
    return summed.astype(jnp.bfloat16)


def spread_back(spread_near, tap_near, count, width):
    summed = jnp.zeros((count, width, spread_near.shape[3]), jnp.float32)
    for north in range(3):
        for east in range(3):
            row_first = 2 - north
            column_first = 2 - east
            weights = tap_near[row_first:row_first + count, 3 * north + east].astype(jnp.float32)
            values = spread_near[row_first:row_first + count, column_first:column_first + width].astype(jnp.float32)
            summed = summed + jnp.einsum('ak,ajkc->ajc', weights, values)
    return summed


def spectral(values, table_in, table_out, before, after, legendre, gain, mixing, adjoint):
    blocks = LATITUDES // CYCLES
    table_in_wide = table_in.astype(jnp.float32)
    table_out_wide = table_out.astype(jnp.float32)

    def analyse(summed, index):
        start = index * CYCLES
        rows = lax.dynamic_slice_in_dim(values, start, CYCLES, 0).astype(jnp.float32)
        modes = jnp.einsum('ajc,jrm->amrc', rows, table_in_wide)
        modes = (modes * lax.dynamic_slice_in_dim(before, start, CYCLES, 0)[:, None, None, None]).astype(jnp.bfloat16)
        degree_rows = lax.dynamic_slice_in_dim(legendre, start, CYCLES, 2).astype(jnp.float32)
        return summed + jnp.einsum('mla,amrc->lmrc', degree_rows, modes.astype(jnp.float32)), None

    summed, unused = lax.scan(analyse, jnp.zeros((DEGREES, ORDERS, 2, CHANNELS), jnp.float32), jnp.arange(blocks, dtype=jnp.int32))
    spectrum = summed.astype(jnp.bfloat16)
    gain_wide = gain.astype(jnp.float32)[:, None, None, :]
    mixing_wide = mixing.astype(jnp.float32)
    if adjoint:
        local = (gain_wide * spectrum.astype(jnp.float32)).astype(jnp.bfloat16)
        mixed = jnp.einsum('lmrf,cf->lmrc', local.astype(jnp.float32), mixing_wide).astype(jnp.bfloat16)
    else:
        local = spectrum
        mixed = (gain_wide * jnp.einsum('lmrc,cf->lmrf', spectrum.astype(jnp.float32), mixing_wide)).astype(jnp.bfloat16)
    mixed_wide = mixed.astype(jnp.float32)

    def synthesize(index):
        start = index * CYCLES
        degree_rows = lax.dynamic_slice_in_dim(legendre, start, CYCLES, 2).astype(jnp.float32)
        cycle_modes = jnp.einsum('mla,lmrc->amrc', degree_rows, mixed_wide).astype(jnp.bfloat16)
        spatial = jnp.einsum('amrc,jrm->ajc', cycle_modes.astype(jnp.float32), table_out_wide)
        return (spatial * lax.dynamic_slice_in_dim(after, start, CYCLES, 0)[:, None, None]).astype(jnp.bfloat16)

    spatial = lax.map(synthesize, jnp.arange(blocks, dtype=jnp.int32)).reshape(LATITUDES, LONGITUDES, CHANNELS)
    return spatial, local


def reference(field, cotangent, legendre, cycle_weight, support_tap, support_basis, support_weight, filter_weight, spectral_weight, spectral_gain):
    blocks = LATITUDES // CYCLES
    tap_all = tap_table(support_tap, support_basis, support_weight)
    tap_padded = jnp.pad(tap_all, ((1, 1), (0, 0), (0, 0)))
    field_padded = jnp.pad(wrap_columns(field), ((1, 1), (0, 0), (0, 0)))
    filter_wide = filter_weight.astype(jnp.float32)

    def forward_block(index):
        start = index * CYCLES
        extended = lax.dynamic_slice_in_dim(field_padded, start, CYCLES + 2, 0)
        filtered = filter_rows(extended, lax.dynamic_slice_in_dim(tap_all, start, CYCLES, 0))
        mixed = jnp.einsum('akjc,kcf->ajf', filtered.astype(jnp.float32), filter_wide)
        own = lax.dynamic_slice_in_dim(field, start, CYCLES, 0).astype(jnp.float32)
        return (own + mixed).astype(jnp.bfloat16)

    hidden = lax.map(forward_block, jnp.arange(blocks, dtype=jnp.int32)).reshape(LATITUDES, LONGITUDES, CHANNELS)
    analysis_table = trig_table(LONGITUDES ** -0.5)
    synthesis_table = trig_table((2 * ORDERS) ** -0.5)
    ones = jnp.ones_like(cycle_weight)
    spatial, spectrum = spectral(hidden, analysis_table, synthesis_table, cycle_weight, ones, legendre, spectral_gain, spectral_weight, False)
    output = (hidden.astype(jnp.float32) + spatial.astype(jnp.float32)).astype(jnp.bfloat16)
    back_spatial, scaled = spectral(cotangent, synthesis_table, analysis_table, ones, cycle_weight, legendre, spectral_gain, spectral_weight, True)
    grad_hidden = (cotangent.astype(jnp.float32) + back_spatial.astype(jnp.float32)).astype(jnp.bfloat16)
    grad_spectral = jnp.einsum('lmrc,lmrf->cf', spectrum.astype(jnp.float32), scaled.astype(jnp.float32)) * (2 * ORDERS * DEGREES) ** -0.5
    grad_padded = jnp.pad(grad_hidden, ((1, 1), (0, 0), (0, 0)))

    def backward_block(summed, index):
        start = index * CYCLES
        near = lax.dynamic_slice_in_dim(grad_padded, start, CYCLES + 2, 0)
        spread = jnp.einsum('ajf,kcf->ajkc', near.astype(jnp.float32), filter_wide).astype(jnp.bfloat16)
        back = spread_back(wrap_columns(spread), lax.dynamic_slice_in_dim(tap_padded, start, CYCLES + 2, 0), CYCLES, LONGITUDES)
        own = lax.dynamic_slice_in_dim(grad_hidden, start, CYCLES, 0).astype(jnp.float32)
        extended = lax.dynamic_slice_in_dim(field_padded, start, CYCLES + 2, 0)
        filtered = filter_rows(extended, lax.dynamic_slice_in_dim(tap_all, start, CYCLES, 0))
        summed = summed + jnp.einsum('akjc,ajf->kcf', filtered.astype(jnp.float32), own)
        return summed, (own + back).astype(jnp.bfloat16)

    summed, grad_blocks = lax.scan(backward_block, jnp.zeros((BASIS_COUNT, CHANNELS, CHANNELS), jnp.float32), jnp.arange(blocks, dtype=jnp.int32))
    grad_field = grad_blocks.reshape(LATITUDES, LONGITUDES, CHANNELS)
    grad_filter = summed * (LATITUDES * LONGITUDES) ** -0.5
    return (output, grad_field, grad_filter, grad_spectral)
```

```python
import functools
import math

import jax
import jax.numpy as jnp
import numpy as np
from jax import lax
from jax.experimental import pallas as pl
from jax.experimental.pallas import tpu as pltpu
from jax.sharding import PartitionSpec as P

LONGITUDES = 768
DEGREES = 384
ORDERS = 16
BASIS_COUNT = 4
LAT = 64
LON = 4
MESH = pl.DeviceIdType.MESH
BF = jnp.bfloat16
F32 = jnp.float32


def with_halo(x, sides, width, wrap):
    for axis, dim in sides:
        devices, length = (lax.axis_size(axis), x.shape[dim])
        up = [(i, (i + 1) % devices) for i in range(devices if wrap else devices - 1)]
        down = [(j, i) for i, j in up]
        last = lax.slice_in_dim(x, length - width, length, axis=dim)
        initial = lax.slice_in_dim(x, 0, width, axis=dim)
        before = lax.ppermute(last, axis, up)
        after = lax.ppermute(initial, axis, down)
        x = jnp.concatenate([before, x, after], axis=dim)
    return x


def tap_table(support_tap, support_basis, support_weight):
    tap_onehot = (support_tap[:, :, None] == jnp.arange(9, dtype=jnp.int32)[None, None, :]).astype(
        jnp.float32
    )
    basis_onehot = (
        support_basis[:, :, None] == jnp.arange(BASIS_COUNT, dtype=jnp.int32)[None, None, :]
    ).astype(jnp.float32)
    table = jnp.einsum(
        "ist,isk->itk",
        tap_onehot * support_weight[:, :, None],
        basis_onehot,
        precision=lax.Precision.HIGHEST,
    )
    return table.astype(jnp.bfloat16)


def trig_table(scale):
    longitude = np.arange(LONGITUDES)
    order = np.arange(ORDERS)
    angle = (longitude[:, None] * order[None, :] % LONGITUDES) * (2.0 * math.pi / LONGITUDES)
    table = np.stack([np.cos(angle), np.sin(angle)], axis=2) * scale
    return table.reshape(LONGITUDES, 2 * ORDERS).astype(np.float32)


def extend_rims(values):
    wider = with_halo(values, (("lon", 1),), 1, True)
    return with_halo(wider, (("lat", 0),), 1, False)


def filter_rows(extended, tap_rows):
    count = extended.shape[0] - 2
    width = extended.shape[1] - 2
    shifted = jnp.stack(
        [
            extended[north : north + count, east : east + width]
            for north in range(3)
            for east in range(3)
        ],
        axis=1,
    )
    return jnp.einsum(
        "atk,atjc->akjc", tap_rows, shifted, preferred_element_type=jnp.float32
    ).astype(jnp.bfloat16)


def spread_back(spread_near, tap_near, count, width):
    summed = jnp.zeros((count, width, spread_near.shape[3]), jnp.float32)
    for north in range(3):
        for east in range(3):
            row_first = 2 - north
            column_first = 2 - east
            weights = tap_near[row_first : row_first + count, 3 * north + east]
            values = spread_near[row_first : row_first + count, column_first : column_first + width]
            summed = summed + jnp.einsum(
                "ak,ajkc->ajc", weights, values, preferred_element_type=jnp.float32
            )
    return summed


def whole_wait(ref, sem):
    pltpu.make_async_copy(ref, ref, sem).wait()


def unpack_constants():
    pick = np.zeros((3, 128, 256), np.float32)
    gain_pick = np.zeros((2, 48, 256), np.float32)
    for dev in range(8):
        for block in range(3):
            for group in range(4):
                for cycle in range(4):
                    pick[block, dev * 16 + group * 4 + cycle, dev * 32 + block * 4 + cycle] = 1.0
        for half in range(2):
            for degree in range(6):
                gain_pick[half, dev * 6 + degree, dev * 32 + 16 + half * 6 + degree] = 1.0
    return pick, gain_pick


def spectral_kernel(
    partial_ref,
    weight_ref,
    legendre_ref,
    gain_ref,
    mixing_ref,
    pick_ref,
    gain_pick_ref,
    cycle_ref,
    term_ref,
    lon_buf,
    gain_buf,
    table_src,
    table_buf,
    mode_src,
    mode_buf,
    rep,
    rep_t,
    gain_all,
    spec,
    scaled_s,
    mixed,
    back_src,
    gain_send,
    gain_recv,
    lon_send,
    lon_recv,
    table_send,
    table_recv,
    mode_send,
    mode_recv,
    back_send,
    back_recv,
    own_sem,
):
    a = lax.axis_index("lat")
    b = lax.axis_index("lon")
    half = lax.div(a, 32)
    slot = lax.rem(a, 32)
    barrier = pltpu.get_barrier_semaphore()

    def greet_lat(d, carry):
        pl.semaphore_signal(
            barrier, inc=1, device_id=(lax.rem(a + d, LAT), b), device_id_type=MESH
        )
        return carry

    for d in range(1, LON):
        pl.semaphore_signal(barrier, inc=1, device_id=(a, lax.rem(b + d, LON)), device_id_type=MESH)
    lax.fori_loop(1, LAT, greet_lat, 0)
    pl.semaphore_wait(barrier, LAT - 1 + LON - 1)

    def to_lon(src, buf, send, recv):
        copies = []
        for d in range(1, LON):
            copy = pltpu.make_async_remote_copy(
                src_ref=src,
                dst_ref=buf.at[d - 1],
                send_sem=send.at[d - 1],
                recv_sem=recv.at[d - 1],
                device_id=(a, lax.rem(b + d, LON)),
                device_id_type=MESH,
            )
            copy.start()
            copies.append(copy)
        return copies

    gain_copies = to_lon(gain_ref, gain_buf, gain_send, gain_recv)
    lon_copies = to_lon(partial_ref, lon_buf, lon_send, lon_recv)

    for copy in gain_copies:
        copy.wait()
    gain_row = gain_ref[...].astype(F32)
    for d in range(LON - 1):
        gain_row = gain_row + gain_buf[d].astype(F32)
    gain_row = gain_row.astype(BF)
    for t in range(ORDERS):
        table_src[t, 0:16, :] = legendre_ref[t]
        table_src[t, 16:32, :] = gain_row

    def send_table(d, carry):
        to = lax.rem(a + d, LAT)
        pltpu.make_async_remote_copy(
            src_ref=table_src.at[lax.div(lax.rem(to, 32), 2)],
            dst_ref=table_buf.at[a],
            send_sem=table_send,
            recv_sem=table_recv,
            device_id=(to, b),
            device_id_type=MESH,
        ).start()
        return carry

    lax.fori_loop(1, LAT, send_table, 0)
    own_table = pltpu.make_async_copy(
        table_src.at[lax.div(slot, 2)], table_buf.at[a], own_sem.at[0]
    )
    own_table.start()

    for copy in lon_copies:
        copy.wait()
    for part in range(4):
        rows = pl.ds(part * 128, 128)
        total = partial_ref[rows, :].astype(F32)
        for d in range(LON - 1):
            total = total + lon_buf[d, rows, :].astype(F32)
        total = total.reshape(8, 16, 128) * weight_ref[...][None]
        mode_src[rows, :] = total.reshape(128, 128).astype(BF)

    def send_modes(d, carry):
        to = lax.rem(a + d, LAT)
        pltpu.make_async_remote_copy(
            src_ref=mode_src.at[pl.ds(pl.multiple_of(lax.rem(to, 32) * 16, 16), 16), :],
            dst_ref=mode_buf.at[pl.ds(pl.multiple_of(a * 16, 16), 16), :],
            send_sem=mode_send,
            recv_sem=mode_recv,
            device_id=(to, b),
            device_id_type=MESH,
        ).start()
        return carry

    lax.fori_loop(1, LAT, send_modes, 0)
    own_modes = pltpu.make_async_copy(
        mode_src.at[pl.ds(pl.multiple_of(slot * 16, 16), 16), :],
        mode_buf.at[pl.ds(pl.multiple_of(a * 16, 16), 16), :],
        own_sem.at[1],
    )
    own_modes.start()

    own_table.wait()
    whole_wait(table_buf.at[pl.ds(0, LAT - 1)], table_recv)
    whole_wait(table_buf.at[pl.ds(0, LAT - 1)], table_send)
    for chunk in range(8):
        packed = table_buf[chunk * 8 : chunk * 8 + 8].reshape(256, 128)
        for block in range(3):
            rows = jnp.dot(pick_ref[block], packed, preferred_element_type=F32)
            rep[chunk * 128 : chunk * 128 + 128, block * 128 : block * 128 + 128] = rows.astype(BF)
            rep_t[block * 128 : block * 128 + 128, chunk * 128 : chunk * 128 + 128] = rows.T.astype(
                BF
            )
        for side in range(2):
            rows = jnp.dot(gain_pick_ref[side], packed, preferred_element_type=F32)
            gain_all[chunk * 48 : chunk * 48 + 48, side * 128 : side * 128 + 128] = rows

    own_modes.wait()
    whole_wait(mode_buf.at[pl.ds(0, 16 * (LAT - 1)), :], mode_recv)
    whole_wait(mode_buf.at[pl.ds(0, 16 * (LAT - 1)), :], mode_send)

    group = lax.rem(lax.div(lax.broadcasted_iota(jnp.int32, (1024, 128), 0), 4), 4)
    modes = mode_buf[...].astype(F32)
    for x in range(4):
        wide = jnp.where(group == x, modes, 0.0).astype(BF)
        spec[:, x * 128 : x * 128 + 128] = jnp.dot(
            rep_t[...], wide, preferred_element_type=F32
        ).astype(BF)
    gains = gain_all[...]
    mixed[:, 0:256] = (
        gains * jnp.dot(spec[:, 0:256], mixing_ref[...], preferred_element_type=F32)
    ).astype(BF)
    scaled_s[...] = (gains * spec[:, 256:512].astype(F32)).astype(BF)
    mixed[:, 256:512] = lax.dot_general(
        scaled_s[...], mixing_ref[...], (((1,), (1,)), ((), ())), preferred_element_type=F32
    ).astype(BF)

    group = lax.rem(lax.div(lax.broadcasted_iota(jnp.int32, (512, 128), 0), 4), 4)
    rows = rep[pl.ds(pl.multiple_of(half * 512, 512), 512), :]
    packed = jnp.zeros((512, 128), F32)
    for x in range(4):
        sums = jnp.dot(rows, mixed[:, x * 128 : x * 128 + 128], preferred_element_type=F32)
        packed = jnp.where(group == x, sums, packed)
    back_src[...] = packed.astype(BF)

    def send_back(d, carry):
        to = lax.rem(slot + d, 32)
        pltpu.make_async_remote_copy(
            src_ref=back_src.at[pl.ds(pl.multiple_of(to * 16, 16), 16), :],
            dst_ref=cycle_ref.at[pl.ds(pl.multiple_of(slot * 16, 16), 16), :],
            send_sem=back_send,
            recv_sem=back_recv,
            device_id=(half * 32 + to, b),
            device_id_type=MESH,
        ).start()
        return carry

    lax.fori_loop(1, 32, send_back, 0)
    own_back = pltpu.make_async_copy(
        back_src.at[pl.ds(pl.multiple_of(slot * 16, 16), 16), :],
        cycle_ref.at[pl.ds(pl.multiple_of(slot * 16, 16), 16), :],
        own_sem.at[2],
    )
    own_back.start()

    degrees = pl.ds(pl.multiple_of((half * 4 + b) * 48, 16), 48)
    term_ref[...] = lax.dot_general(
        spec[degrees, 0:256],
        scaled_s[degrees, :],
        (((0,), (0,)), ((), ())),
        preferred_element_type=F32,
    )
    own_back.wait()
    whole_wait(cycle_ref.at[pl.ds(0, 16 * 31), :], back_recv)
    whole_wait(cycle_ref.at[pl.ds(0, 16 * 31), :], back_send)


def spectral_call(partial, weight, legendre, gain, mixing):
    pick, gain_pick = unpack_constants()
    vmem = pl.BlockSpec(memory_space=pltpu.VMEM)
    dma = pltpu.SemaphoreType.DMA
    return pl.pallas_call(
        spectral_kernel,
        out_shape=(
            jax.ShapeDtypeStruct((512, 128), BF),
            jax.ShapeDtypeStruct((256, 256), F32),
        ),
        in_specs=[vmem] * 7,
        out_specs=(vmem, vmem),
        scratch_shapes=[
            pltpu.VMEM((3, 512, 128), BF),
            pltpu.VMEM((3, 16, 128), BF),
            pltpu.VMEM((16, 32, 128), BF),
            pltpu.VMEM((LAT, 32, 128), BF),
            pltpu.VMEM((512, 128), BF),
            pltpu.VMEM((1024, 128), BF),
            pltpu.VMEM((1024, DEGREES), BF),
            pltpu.VMEM((DEGREES, 1024), BF),
            pltpu.VMEM((DEGREES, 256), F32),
            pltpu.VMEM((DEGREES, 512), BF),
            pltpu.VMEM((DEGREES, 256), BF),
            pltpu.VMEM((DEGREES, 512), BF),
            pltpu.VMEM((512, 128), BF),
            dma((3,)),
            dma((3,)),
            dma((3,)),
            dma((3,)),
            dma,
            dma,
            dma,
            dma,
            dma,
            dma,
            dma((3,)),
        ],
        compiler_params=pltpu.CompilerParams(
            collective_id=0, has_side_effects=True, vmem_limit_bytes=40 * 2**20
        ),
        name="spectral",
    )(partial, weight, legendre, gain, mixing, jnp.asarray(pick, BF), jnp.asarray(gain_pick, BF))


ROWS = 1280
PIECE = 80


def reduce_kernel(
    x_ref,
    out_ref,
    core_src,
    core_buf,
    plane_src,
    plane_buf,
    z_buf,
    whole_buf,
    core_send,
    core_recv,
    plane_send,
    plane_recv,
    z_send,
    z_recv,
    back_send,
    back_recv,
    last_send,
    last_recv,
    own_sem,
):
    a = lax.axis_index("lat")
    b = lax.axis_index("lon")
    x = lax.rem(a, 4)
    y_lo = lax.rem(lax.div(a, 4), 2)
    z = lax.div(a, 8)
    core = lax.rem(b, 2)
    y = lax.div(b, 2) * 2 + y_lo
    place = y * 4 + x
    other_core = lax.div(b, 2) * 2 + 1 - core
    barrier = pltpu.get_barrier_semaphore()

    def plane_peer(g):
        py, px = lax.div(g, 4), lax.rem(g, 4)
        return (z * 8 + lax.rem(py, 2) * 4 + px, lax.div(py, 2) * 2 + core)

    def z_peer(g):
        return (g * 8 + y_lo * 4 + x, b)

    def greet_plane(d, carry):
        pl.semaphore_signal(
            barrier, inc=1, device_id=plane_peer(lax.rem(place + d, 16)), device_id_type=MESH
        )
        return carry

    def greet_z(d, carry):
        pl.semaphore_signal(
            barrier, inc=1, device_id=z_peer(lax.rem(z + d, 8)), device_id_type=MESH
        )
        return carry

    pl.semaphore_signal(barrier, inc=1, device_id=(a, other_core), device_id_type=MESH)
    lax.fori_loop(1, 16, greet_plane, 0)
    lax.fori_loop(1, 8, greet_z, 0)
    pl.semaphore_wait(barrier, 1 + 15 + 7)

    core_src[...] = x_ref[1 - core].astype(BF)
    copy = pltpu.make_async_remote_copy(
        src_ref=core_src,
        dst_ref=core_buf,
        send_sem=core_send,
        recv_sem=core_recv,
        device_id=(a, other_core),
        device_id_type=MESH,
    )
    copy.start()
    copy.wait()
    plane_src[...] = (x_ref[core] + core_buf[...].astype(F32)).astype(BF)

    def send_plane(d, carry):
        g = lax.rem(place + d, 16)
        pltpu.make_async_remote_copy(
            src_ref=plane_src.at[pl.ds(pl.multiple_of(g * PIECE, 16), PIECE), :],
            dst_ref=plane_buf.at[place],
            send_sem=plane_send,
            recv_sem=plane_recv,
            device_id=plane_peer(g),
            device_id_type=MESH,
        ).start()
        return carry

    lax.fori_loop(1, 16, send_plane, 0)
    own = pltpu.make_async_copy(
        plane_src.at[pl.ds(pl.multiple_of(place * PIECE, 16), PIECE), :],
        plane_buf.at[place],
        own_sem.at[0],
    )
    own.start()
    own.wait()
    whole_wait(plane_buf.at[pl.ds(0, 15)], plane_recv)
    whole_wait(plane_buf.at[pl.ds(0, 15)], plane_send)
    total = plane_buf[0].astype(F32)
    for g in range(1, 16):
        total = total + plane_buf[g].astype(F32)
    z_buf[z] = total.astype(BF)

    def send_z(d, carry):
        g = lax.rem(z + d, 8)
        pltpu.make_async_remote_copy(
            src_ref=z_buf.at[z],
            dst_ref=z_buf.at[z],
            send_sem=z_send,
            recv_sem=z_recv,
            device_id=z_peer(g),
            device_id_type=MESH,
        ).start()
        return carry

    lax.fori_loop(1, 8, send_z, 0)
    whole_wait(z_buf.at[pl.ds(0, 7)], z_recv)
    whole_wait(z_buf.at[pl.ds(0, 7)], z_send)
    total = z_buf[0].astype(F32)
    for g in range(1, 8):
        total = total + z_buf[g].astype(F32)
    mine = pl.ds(pl.multiple_of(place * PIECE, 16), PIECE)
    whole_buf[core, mine, :] = total.astype(BF)

    def send_piece(d, carry):
        pltpu.make_async_remote_copy(
            src_ref=whole_buf.at[core, mine, :],
            dst_ref=whole_buf.at[core, mine, :],
            send_sem=back_send,
            recv_sem=back_recv,
            device_id=plane_peer(lax.rem(place + d, 16)),
            device_id_type=MESH,
        ).start()
        return carry

    lax.fori_loop(1, 16, send_piece, 0)
    whole_wait(whole_buf.at[core, pl.ds(0, 15 * PIECE), :], back_recv)
    whole_wait(whole_buf.at[core, pl.ds(0, 15 * PIECE), :], back_send)
    copy = pltpu.make_async_remote_copy(
        src_ref=whole_buf.at[core],
        dst_ref=whole_buf.at[core],
        send_sem=last_send,
        recv_sem=last_recv,
        device_id=(a, other_core),
        device_id_type=MESH,
    )
    copy.start()
    copy.wait()
    out_ref[...] = whole_buf[...].astype(F32)


def reduce_call(x):
    vmem = pl.BlockSpec(memory_space=pltpu.VMEM)
    dma = pltpu.SemaphoreType.DMA
    return pl.pallas_call(
        reduce_kernel,
        out_shape=jax.ShapeDtypeStruct((2, ROWS, 128), F32),
        in_specs=[vmem],
        out_specs=vmem,
        scratch_shapes=[
            pltpu.VMEM((ROWS, 128), BF),
            pltpu.VMEM((ROWS, 128), BF),
            pltpu.VMEM((ROWS, 128), BF),
            pltpu.VMEM((16, PIECE, 128), BF),
            pltpu.VMEM((8, PIECE, 128), BF),
            pltpu.VMEM((2, ROWS, 128), BF),
        ]
        + [dma] * 10
        + [dma((1,))],
        compiler_params=pltpu.CompilerParams(
            collective_id=1, has_side_effects=True, vmem_limit_bytes=40 * 2**20
        ),
        name="reduce",
    )(x)


def per_device(
    field,
    cotangent,
    legendre,
    cycle_weight,
    support_tap,
    support_basis,
    support_weight,
    filter_weight,
    spectral_weight,
    spectral_gain,
):
    cycle_count, width, channels = field.shape
    cycle_start = lax.axis_index("lat") * cycle_count
    lon = lax.axis_index("lon")
    tap_all = tap_table(support_tap, support_basis, support_weight)
    tap_padded = jnp.pad(tap_all, ((1, 1), (0, 0), (0, 0)))
    tap_own = lax.dynamic_slice_in_dim(tap_all, cycle_start, cycle_count, 0)
    tap_near = lax.dynamic_slice_in_dim(tap_padded, cycle_start, cycle_count + 2, 0)
    filtered = filter_rows(extend_rims(field), tap_own)
    filter_out = jnp.einsum(
        "akjc,kcf->ajf", filtered, filter_weight, preferred_element_type=jnp.float32
    )
    hidden = (field.astype(jnp.float32) + filter_out).astype(jnp.bfloat16)
    analysis = jnp.asarray(trig_table(LONGITUDES ** (-0.5)), BF).reshape(LON, width, 32)[lon]
    synthesis = jnp.asarray(trig_table((2 * ORDERS) ** (-0.5)), BF).reshape(LON, width, 32)[lon]

    fore = jnp.einsum("ajc,jm->mac", hidden, analysis, preferred_element_type=F32)
    back = jnp.einsum("ajc,jm->mac", cotangent, synthesis, preferred_element_type=F32)
    partial = jnp.stack([fore, back], axis=1).reshape(32, 2, 4, 2, 128)
    partial = partial.transpose(0, 1, 3, 2, 4).reshape(512, 128).astype(BF)
    ones = jnp.ones((2, 4), F32)
    weight = jnp.stack([jnp.broadcast_to(cycle_weight, (2, 4)), ones]).reshape(16, 1)
    weight = jnp.broadcast_to(weight, (16, 128))
    table = legendre.reshape(16, 3, 128, 4).transpose(0, 1, 3, 2).reshape(16, 12, 128)
    table = jnp.pad(table, ((0, 0), (0, 4), (0, 0)))
    at = jnp.arange(4, dtype=jnp.int32) == lon
    gain = jnp.where(at[None, :, None], spectral_gain[:, None, :], 0).reshape(6, 2, 128)
    gain = jnp.pad(gain.transpose(1, 0, 2).reshape(12, 128), ((0, 4), (0, 0)))
    cycles, spectral_term = spectral_call(partial, weight, table, gain, spectral_weight)
    cycles = cycles.reshape(32, 2, 2, 4, 128)
    fore_cycles, back_cycles = cycles[:, 0], cycles[:, 1]

    spatial = jnp.einsum("mhax,jm->ajhx", fore_cycles, synthesis, preferred_element_type=F32)
    spatial = spatial.reshape(4, width, 256).astype(BF)
    output = (hidden.astype(jnp.float32) + spatial.astype(jnp.float32)).astype(jnp.bfloat16)
    back_spatial = jnp.einsum("mhax,jm->ajhx", back_cycles, analysis, preferred_element_type=F32)
    back_spatial = (back_spatial.reshape(4, width, 256) * cycle_weight[:, None, None]).astype(BF)
    grad_hidden = (cotangent.astype(jnp.float32) + back_spatial.astype(jnp.float32)).astype(
        jnp.bfloat16
    )
    spread = jnp.einsum(
        "ajf,kcf->ajkc", grad_hidden, filter_weight, preferred_element_type=jnp.float32
    ).astype(jnp.bfloat16)
    spread_near = extend_rims(spread)
    back_filter = spread_back(spread_near, tap_near, cycle_count, width)
    grad_field = (grad_hidden.astype(jnp.float32) + back_filter).astype(jnp.bfloat16)
    filter_term = jnp.einsum("akjc,ajf->kcf", filtered, grad_hidden, preferred_element_type=F32)
    terms = jnp.concatenate([filter_term.reshape(1024, 256), spectral_term])
    sums = reduce_call(terms.reshape(ROWS, 2, 128).transpose(1, 0, 2))
    sums = sums.transpose(1, 0, 2).reshape(ROWS, 256)
    grid_scale = (cycle_count * lax.axis_size("lat") * LONGITUDES) ** (-0.5)
    grad_filter = sums[:1024].reshape(4, 256, 256) * grid_scale
    spectral_sum = sums[1024:] * (2 * ORDERS * DEGREES) ** (-0.5)
    grad_spectral = lax.dynamic_slice_in_dim(spectral_sum, lon * 64, 64, 1)
    return (output, grad_field, grad_filter, grad_spectral)


def solution(mesh):
    placed = (
        P("lat", "lon", None),
        P("lat", "lon", None),
        P(None, None, "lat"),
        P("lat"),
        P(),
        P(),
        P(),
        P(),
        P(),
        P("lat", "lon"),
    )
    return jax.shard_map(
        per_device,
        mesh=mesh,
        in_specs=placed,
        out_specs=(P("lat", "lon", None), P("lat", "lon", None), P(), P(None, "lon")),
        check_vma=False,
    )
```

```python
import math

import jax
import jax.numpy as jnp
import numpy as np
from jax import lax
from jax.experimental import pallas as pl
from jax.experimental.pallas import tpu as pltpu
from jax.sharding import PartitionSpec as P

LATITUDES = 256
LONGITUDES = 768
DEGREES = 384
ORDERS = 16
BASIS_COUNT = 4
LAT = 64
LON = 4
WIDTH = LONGITUDES // LON
WIDE = WIDTH + 32
ROWS = 1280
PIECE = 80
MESH = pl.DeviceIdType.MESH
BF = jnp.bfloat16
F32 = jnp.float32


def trig_tables():
    longitude = np.arange(LONGITUDES)
    order = np.arange(ORDERS)
    angle = (longitude[:, None] * order[None, :] % LONGITUDES) * (2.0 * math.pi / LONGITUDES)
    table = np.stack([np.cos(angle), np.sin(angle)], axis=2).reshape(LONGITUDES, 2 * ORDERS)
    both = np.stack([table * LONGITUDES ** (-0.5), table * (2 * ORDERS) ** (-0.5)])
    both = both.astype(np.float32)
    where = np.arange(LON)[:, None] * WIDTH + np.arange(-16, WIDTH + 16)[None, :]
    wide = both[:, where % LONGITUDES].transpose(1, 0, 2, 3)
    across = wide[:, :, 16 : 16 + WIDTH].transpose(0, 1, 3, 2)
    return wide, across


def whole_wait(ref, sem):
    pltpu.make_async_copy(ref, ref, sem).wait()


def unpack_constants():
    pick = np.zeros((3, 128, 256), np.float32)
    gain_pick = np.zeros((2, 48, 256), np.float32)
    for dev in range(8):
        for block in range(3):
            for group in range(4):
                for cycle in range(4):
                    pick[block, dev * 16 + group * 4 + cycle, dev * 32 + block * 4 + cycle] = 1.0
        for half in range(2):
            for degree in range(6):
                gain_pick[half, dev * 6 + degree, dev * 32 + 16 + half * 6 + degree] = 1.0
    return pick, gain_pick


def block_kernel(
    tap_ref,
    cycle_weight_ref,
    field_ref,
    cot_ref,
    legendre_ref,
    gain_ref,
    mixing_ref,
    filter_ref,
    pick_ref,
    gain_pick_ref,
    wide_ref,
    across_ref,
    out_ref,
    grad_ref,
    grad_filter_ref,
    grad_spectral_ref,
    field_wide,
    cot_wide,
    grad_wide,
    band,
    band_back,
    filtered,
    filtered_t,
    hidden,
    grad_own,
    partial,
    partial_src,
    lon_buf,
    gain_buf,
    table_src,
    table_buf,
    mode_src,
    mode_buf,
    rep,
    rep_t,
    gain_all,
    spec,
    scaled_s,
    mixed,
    back_src,
    cycle_buf,
    cycle_wide,
    fore_cycles,
    near_cycles,
    terms,
    core_src,
    core_buf,
    plane_src,
    plane_buf,
    z_buf,
    whole_buf,
    sem,
    lon_sem,
    near_sem,
):
    a = lax.axis_index("lat")
    b = lax.axis_index("lon")
    half = lax.div(a, 32)
    slot = lax.rem(a, 32)
    x = lax.rem(a, 4)
    y_lo = lax.rem(lax.div(a, 4), 2)
    z = lax.div(a, 8)
    core = lax.rem(b, 2)
    y_hi = lax.div(b, 2)
    place = (y_hi * 2 + y_lo) * 4 + x
    other_core = y_hi * 2 + 1 - core
    north, south = lax.rem(a + LAT - 1, LAT), lax.rem(a + 1, LAT)
    west, east = lax.rem(b + LON - 1, LON), lax.rem(b + 1, LON)
    barrier = pltpu.get_barrier_semaphore()

    def plane_peer(g):
        py, px = lax.div(g, 4), lax.rem(g, 4)
        return (z * 8 + lax.rem(py, 2) * 4 + px, lax.div(py, 2) * 2 + core)

    def z_peer(g):
        return (g * 8 + y_lo * 4 + x, b)

    def greet(device):
        pl.semaphore_signal(barrier, inc=1, device_id=device, device_id_type=MESH)

    def greet_lat(d, carry):
        greet((lax.rem(a + d, LAT), b))
        return carry

    def greet_far(d, carry):
        g = lax.rem(lax.rem(place, 8) + d, 8)
        greet((z * 8 + g, (1 - y_hi) * 2 + core))
        return carry

    for d in range(1, LON):
        greet((a, lax.rem(b + d, LON)))
    for lat in (north, south):
        for lon in (west, east):
            greet((lat, lon))
    lax.fori_loop(1, 8, greet_far, 0)
    lax.fori_loop(1, LAT, greet_lat, 0)

    def send(src, dst, send_sem, recv_sem, device):
        copy = pltpu.make_async_remote_copy(
            src_ref=src,
            dst_ref=dst,
            send_sem=send_sem,
            recv_sem=recv_sem,
            device_id=device,
            device_id_type=MESH,
        )
        copy.start()
        return copy

    field_wide[1:5, 16 : 16 + WIDTH, :] = field_ref[...]
    cot_wide[1:5, 16 : 16 + WIDTH, :] = cot_ref[...]

    def pack_partial(which, table, rows):
        for i in range(4):
            sums = jnp.dot(across_ref[b, table], rows[i], preferred_element_type=F32)
            for h in range(2):
                partial[which, pl.ds(h * 4 + i, 32, stride=8), :] = sums[:, h * 128 : h * 128 + 128]
        partial_src[which] = partial[which].astype(BF)

    pack_partial(1, 1, cot_ref)
    pl.semaphore_wait(barrier, LAT - 1 + LON - 1 + 4 + 7)

    def send_rims(src, dst, send_sem, recv_sem):
        last, first = pl.ds(WIDTH - 16, 16), pl.ds(0, 16)
        left, right, middle = pl.ds(0, 16), pl.ds(WIDTH + 16, 16), pl.ds(16, WIDTH)
        send(src.at[3], dst.at[0, middle, :], send_sem, recv_sem, (south, b))
        send(src.at[0], dst.at[5, middle, :], send_sem, recv_sem, (north, b))
        inner = pl.ds(1, 4)
        send(src.at[:, last, :], dst.at[inner, left, :], send_sem, recv_sem, (a, east))
        send(src.at[:, first, :], dst.at[inner, right, :], send_sem, recv_sem, (a, west))
        send(src.at[3, last, :], dst.at[0, left, :], send_sem, recv_sem, (south, east))
        send(src.at[3, first, :], dst.at[0, right, :], send_sem, recv_sem, (south, west))
        send(src.at[0, last, :], dst.at[5, left, :], send_sem, recv_sem, (north, east))
        send(src.at[0, first, :], dst.at[5, right, :], send_sem, recv_sem, (north, west))

    def rims_size(dst):
        return dst.at[pl.ds(0, 3), pl.ds(0, WIDTH), :]

    def to_lon(src, buf, kind):
        return [
            send(
                src,
                buf.at[d - 1],
                lon_sem.at[kind, 0, d - 1],
                lon_sem.at[kind, 1, d - 1],
                (a, lax.rem(b + d, LON)),
            )
            for d in range(1, LON)
        ]

    send_rims(field_ref, field_wide, sem.at[0], sem.at[1])
    gain_copies = to_lon(gain_ref, gain_buf, 0)
    back_copies = to_lon(partial_src.at[1], lon_buf.at[1], 1)

    diagonal = lax.broadcasted_iota(jnp.int32, (96, 128), 1)
    diagonal = diagonal - lax.broadcasted_iota(jnp.int32, (96, 128), 0) - 15
    inside_north = jnp.where(a == 0, 0.0, 1.0)
    inside_south = jnp.where(a == LAT - 1, 0.0, 1.0)

    def make_band(dst, i, adjoint):
        for p in range(3):
            for k in range(BASIS_COUNT):
                block = jnp.zeros((96, 128), F32)
                for q in range(3):
                    if adjoint:
                        value = tap_ref[i + p, (8 - 3 * p - q) * BASIS_COUNT + k]
                    else:
                        value = tap_ref[i + 1, (3 * p + q) * BASIS_COUNT + k]
                        if i == 0 and p == 0:
                            value = value * inside_north
                        if i == 3 and p == 2:
                            value = value * inside_south
                    block = jnp.where(diagonal == q, value, block)
                dst[i, k * 96 : k * 96 + 96, p * 128 : p * 128 + 128] = block.astype(BF)

    for i in range(4):
        make_band(band, i, False)

    for copy in gain_copies:
        copy.wait()
    gain_row = gain_ref[...].astype(F32)
    for d in range(LON - 1):
        gain_row = gain_row + gain_buf[d].astype(F32)
    gain_row = gain_row.astype(BF)
    for t in range(ORDERS):
        table_src[t, 0:16, :] = legendre_ref[t]
        table_src[t, 16:32, :] = gain_row

    def send_table(d, carry):
        to = lax.rem(a + d, LAT)
        src = table_src.at[lax.div(lax.rem(to, 32), 2)]
        send(src, table_buf.at[a], sem.at[2], sem.at[3], (to, b))
        return carry

    lax.fori_loop(1, LAT, send_table, 0)
    own_table = pltpu.make_async_copy(
        table_src.at[lax.div(slot, 2)], table_buf.at[a], sem.at[4]
    )
    own_table.start()

    def stencil(src, bands, i, block):
        near = jnp.concatenate([src[i + p, block * 96 : block * 96 + 128, :] for p in range(3)])
        return jnp.dot(bands[i], near, preferred_element_type=F32).astype(BF)

    whole_wait(rims_size(field_wide), sem.at[1])
    for i in range(4):
        for block in range(2):
            sums = stencil(field_wide, band, i, block)
            first = i * WIDTH + block * 96
            for k in range(BASIS_COUNT):
                filtered[first : first + 96, k * 256 : k * 256 + 256] = sums[k * 96 : k * 96 + 96]
        own = slice(i * WIDTH, i * WIDTH + WIDTH)
        mix = jnp.dot(filtered[own, :], filter_ref[...], preferred_element_type=F32)
        hidden[i] = (field_ref[i].astype(F32) + mix).astype(BF)
    pack_partial(0, 0, hidden)
    fore_copies = to_lon(partial_src.at[0], lon_buf.at[0], 2)
    send_rims(cot_ref, cot_wide, sem.at[5], sem.at[6])

    own_table.wait()
    whole_wait(table_buf.at[pl.ds(0, LAT - 1)], sem.at[3])
    for chunk in range(8):
        packed = table_buf[chunk * 8 : chunk * 8 + 8].reshape(256, 128)
        for block in range(3):
            rows = jnp.dot(pick_ref[block], packed, preferred_element_type=F32)
            rep[chunk * 128 : chunk * 128 + 128, block * 128 : block * 128 + 128] = rows.astype(BF)
            rep_t[block * 128 : block * 128 + 128, chunk * 128 : chunk * 128 + 128] = rows.T.astype(
                BF
            )
        for side in range(2):
            rows = jnp.dot(gain_pick_ref[side], packed, preferred_element_type=F32)
            gain_all[chunk * 48 : chunk * 48 + 48, side * 128 : side * 128 + 128] = rows

    for copy in back_copies + fore_copies:
        copy.wait()
    cycle = lax.rem(lax.broadcasted_iota(jnp.int32, (8, 128), 0), 4)
    weight = jnp.zeros((8, 128), F32)
    for i in range(4):
        weight = jnp.where(cycle == i, cycle_weight_ref[i], weight)
    for part in range(4):
        rows = pl.ds(part * 64, 64)
        totals = []
        for which in range(2):
            total = partial_src[which, rows, :].astype(F32)
            for d in range(LON - 1):
                total = total + lon_buf[which, d, rows, :].astype(F32)
            totals.append(total.reshape(8, 8, 128))
        total = jnp.concatenate([totals[0] * weight[None], totals[1]], axis=1)
        mode_src[pl.ds(part * 128, 128), :] = total.reshape(128, 128).astype(BF)

    def tile(index):
        return pl.ds(pl.multiple_of(index * 16, 16), 16)

    def send_modes(d, carry):
        to = lax.rem(a + d, LAT)
        src = mode_src.at[tile(lax.rem(to, 32)), :]
        send(src, mode_buf.at[tile(a), :], sem.at[7], sem.at[8], (to, b))
        return carry

    lax.fori_loop(1, LAT, send_modes, 0)
    own_modes = pltpu.make_async_copy(
        mode_src.at[tile(slot), :], mode_buf.at[tile(a), :], sem.at[9]
    )
    own_modes.start()

    for k in range(BASIS_COUNT):
        for pair in range(2):
            rows = filtered[pair * 384 : pair * 384 + 384, k * 256 : k * 256 + 256]
            filtered_t[k * 256 : k * 256 + 256, pair * 384 : pair * 384 + 384] = rows.T
    for i in range(4):
        make_band(band_back, i, True)

    own_modes.wait()
    whole_wait(mode_buf.at[pl.ds(0, 16 * (LAT - 1)), :], sem.at[8])
    group = lax.rem(lax.div(lax.broadcasted_iota(jnp.int32, (1024, 128), 0), 4), 4)
    modes = mode_buf[...].astype(F32)
    for g in range(4):
        kept = jnp.where(group == g, modes, 0.0).astype(BF)
        spec[:, g * 128 : g * 128 + 128] = jnp.dot(
            rep_t[...], kept, preferred_element_type=F32
        ).astype(BF)
    gains = gain_all[...]
    mixed[:, 0:256] = (
        gains * jnp.dot(spec[:, 0:256], mixing_ref[...], preferred_element_type=F32)
    ).astype(BF)
    scaled_s[...] = (gains * spec[:, 256:512].astype(F32)).astype(BF)
    mixed[:, 256:512] = lax.dot_general(
        scaled_s[...], mixing_ref[...], (((1,), (1,)), ((), ())), preferred_element_type=F32
    ).astype(BF)
    group = lax.rem(lax.div(lax.broadcasted_iota(jnp.int32, (512, 128), 0), 4), 4)
    rows = rep[pl.ds(pl.multiple_of(half * 512, 512), 512), :]
    packed = jnp.zeros((512, 128), F32)
    for g in range(4):
        sums = jnp.dot(rows, mixed[:, g * 128 : g * 128 + 128], preferred_element_type=F32)
        packed = jnp.where(group == g, sums, packed)
    back_src[...] = packed.astype(BF)

    def send_back(d, carry):
        to = lax.rem(slot + d, 32)
        src = back_src.at[tile(to), :]
        dst = cycle_buf.at[tile(slot), :]
        send(src, dst, sem.at[10], sem.at[11], (half * 32 + to, b))
        return carry

    lax.fori_loop(1, 32, send_back, 0)
    own_back = pltpu.make_async_copy(
        back_src.at[tile(slot), :], cycle_buf.at[tile(slot), :], sem.at[12]
    )
    own_back.start()

    degrees = pl.ds(pl.multiple_of((half * 4 + b) * 48, 16), 48)
    term = lax.dot_general(
        spec[degrees, 0:256],
        scaled_s[degrees, :],
        (((0,), (0,)), ((), ())),
        preferred_element_type=F32,
    )
    for h in range(2):
        terms[h, 1024:1280, :] = term[:, h * 128 : h * 128 + 128]

    own_back.wait()
    whole_wait(cycle_buf.at[pl.ds(0, 16 * 31), :], sem.at[11])
    cycle_wide[...] = cycle_buf[...].astype(F32)

    def cycle_rows(which, i):
        return jnp.concatenate(
            [cycle_wide[pl.ds(which * 8 + h * 4 + i, 32, stride=16), :] for h in range(2)], axis=1
        )

    for i in (0, 3, 1, 2):
        near_cycles[i + 1] = (cycle_rows(1, i) * cycle_weight_ref[i]).astype(BF)
    near_copies = [
        send(near_cycles.at[1], near_cycles.at[5], near_sem.at[0], near_sem.at[1], (north, b)),
        send(near_cycles.at[4], near_cycles.at[0], near_sem.at[2], near_sem.at[3], (south, b)),
    ]

    def make_grad(r):
        spatial = jnp.dot(wide_ref[b, 0], near_cycles[r], preferred_element_type=F32).astype(BF)
        return (cot_wide[r].astype(F32) + spatial.astype(F32)).astype(BF)

    whole_wait(rims_size(cot_wide), sem.at[6])
    for i in range(4):
        grad = make_grad(i + 1)
        grad_wide[i + 1] = grad
        grad_own[i * WIDTH : i * WIDTH + WIDTH, :] = grad[16 : 16 + WIDTH]
    for k in range(BASIS_COUNT):
        own = slice(k * 256, k * 256 + 256)
        term = jnp.dot(filtered_t[own, :], grad_own[...], preferred_element_type=F32)
        for h in range(2):
            terms[h, own, :] = term[:, h * 128 : h * 128 + 128]

    core_src[...] = terms[1 - core].astype(BF)
    core_copy = send(core_src, core_buf, sem.at[13], sem.at[14], (a, other_core))

    for i in range(4):
        fore_cycles[i] = cycle_rows(0, i).astype(BF)
    for i in range(4):
        spatial = jnp.dot(
            wide_ref[b, 1, 16 : 16 + WIDTH, :], fore_cycles[i], preferred_element_type=F32
        ).astype(BF)
        out_ref[i] = (hidden[i].astype(F32) + spatial.astype(F32)).astype(BF)

    core_copy.wait()
    plane_src[...] = (terms[core] + core_buf[...].astype(F32)).astype(BF)

    def piece(g):
        return pl.ds(pl.multiple_of(g * PIECE, 16), PIECE)

    def send_plane(d, carry):
        g = lax.rem(place + d, 16)
        send(
            plane_src.at[piece(g), :], plane_buf.at[place], sem.at[15], sem.at[16], plane_peer(g)
        )
        return carry

    lax.fori_loop(1, 16, send_plane, 0)
    own_piece = pltpu.make_async_copy(
        plane_src.at[piece(place), :], plane_buf.at[place], sem.at[17]
    )
    own_piece.start()

    for copy in near_copies:
        copy.wait()
    for r in (0, 5):
        grad_wide[r] = make_grad(r)

    def field_grad(i):
        total = grad_own[i * WIDTH : i * WIDTH + WIDTH, :].astype(F32)
        parts = []
        for block in range(2):
            sums = stencil(grad_wide, band_back, i, block)
            part = total[block * 96 : block * 96 + 96]
            for k in range(BASIS_COUNT):
                part = part + lax.dot_general(
                    sums[k * 96 : k * 96 + 96],
                    filter_ref[k * 256 : k * 256 + 256, :],
                    (((1,), (1,)), ((), ())),
                    preferred_element_type=F32,
                )
            parts.append(part)
        grad_ref[i] = jnp.concatenate(parts).astype(BF)

    field_grad(0)
    field_grad(1)

    own_piece.wait()
    whole_wait(plane_buf.at[pl.ds(0, 15)], sem.at[16])
    total = plane_buf[0].astype(F32)
    for g in range(1, 16):
        total = total + plane_buf[g].astype(F32)
    z_buf[z] = total.astype(BF)

    def send_z(d, carry):
        send(z_buf.at[z], z_buf.at[z], sem.at[18], sem.at[19], z_peer(lax.rem(z + d, 8)))
        return carry

    lax.fori_loop(1, 8, send_z, 0)
    field_grad(2)
    whole_wait(z_buf.at[pl.ds(0, 7)], sem.at[19])
    total = z_buf[0].astype(F32)
    for g in range(1, 8):
        total = total + z_buf[g].astype(F32)
    mine = whole_buf.at[core, piece(place), :]
    whole_buf[core, piece(place), :] = total.astype(BF)

    def send_piece(d, carry):
        send(mine, mine, sem.at[20], sem.at[21], plane_peer(lax.rem(place + d, 16)))
        return carry

    lax.fori_loop(1, 16, send_piece, 0)
    field_grad(3)
    whole_wait(whole_buf.at[core, pl.ds(0, 15 * PIECE), :], sem.at[21])
    whole_wait(whole_buf.at[core, pl.ds(0, 15 * PIECE), :], sem.at[20])
    last_copy = send(
        whole_buf.at[core], whole_buf.at[core], sem.at[22], sem.at[23], (a, other_core)
    )

    whole_wait(rims_size(field_wide), sem.at[0])
    whole_wait(table_buf.at[pl.ds(0, LAT - 1)], sem.at[2])
    whole_wait(rims_size(cot_wide), sem.at[5])
    whole_wait(mode_buf.at[pl.ds(0, 16 * (LAT - 1)), :], sem.at[7])
    whole_wait(cycle_buf.at[pl.ds(0, 16 * 31), :], sem.at[10])
    whole_wait(plane_buf.at[pl.ds(0, 15)], sem.at[15])
    whole_wait(z_buf.at[pl.ds(0, 7)], sem.at[18])
    last_copy.wait()

    grid_scale = (LATITUDES * LONGITUDES) ** (-0.5)
    for h in range(2):
        lanes = slice(h * 128, h * 128 + 128)
        grad_filter_ref[:, lanes] = whole_buf[h, 0:1024, :].astype(F32) * grid_scale
    columns = whole_buf[y_hi, 1024:1280, :].astype(F32) * (2 * ORDERS * DEGREES) ** (-0.5)
    grad_spectral_ref[...] = jnp.where(core == 0, columns[:, 0:64], columns[:, 64:128])


def block_call(taps, cycle_weight, field, cotangent, legendre, gain, mixing, filter_weight):
    pick, gain_pick = unpack_constants()
    wide, across = trig_tables()
    vmem = pl.BlockSpec(memory_space=pltpu.VMEM)
    smem = pl.BlockSpec(memory_space=pltpu.SMEM)
    dma = pltpu.SemaphoreType.DMA
    return pl.pallas_call(
        block_kernel,
        out_shape=(
            jax.ShapeDtypeStruct((4, WIDTH, 256), BF),
            jax.ShapeDtypeStruct((4, WIDTH, 256), BF),
            jax.ShapeDtypeStruct((1024, 256), F32),
            jax.ShapeDtypeStruct((256, 64), F32),
        ),
        in_specs=[smem] * 2 + [vmem] * 10,
        out_specs=(vmem,) * 4,
        scratch_shapes=[
            pltpu.VMEM((6, WIDE, 256), BF),
            pltpu.VMEM((6, WIDE, 256), BF),
            pltpu.VMEM((6, WIDE, 256), BF),
            pltpu.VMEM((4, 384, 384), BF),
            pltpu.VMEM((4, 384, 384), BF),
            pltpu.VMEM((768, 1024), BF),
            pltpu.VMEM((1024, 768), BF),
            pltpu.VMEM((4, WIDTH, 256), BF),
            pltpu.VMEM((768, 256), BF),
            pltpu.VMEM((2, 256, 128), F32),
            pltpu.VMEM((2, 256, 128), BF),
            pltpu.VMEM((2, 3, 256, 128), BF),
            pltpu.VMEM((3, 16, 128), BF),
            pltpu.VMEM((16, 32, 128), BF),
            pltpu.VMEM((LAT, 32, 128), BF),
            pltpu.VMEM((512, 128), BF),
            pltpu.VMEM((1024, 128), BF),
            pltpu.VMEM((1024, DEGREES), BF),
            pltpu.VMEM((DEGREES, 1024), BF),
            pltpu.VMEM((DEGREES, 256), F32),
            pltpu.VMEM((DEGREES, 512), BF),
            pltpu.VMEM((DEGREES, 256), BF),
            pltpu.VMEM((DEGREES, 512), BF),
            pltpu.VMEM((512, 128), BF),
            pltpu.VMEM((512, 128), BF),
            pltpu.VMEM((512, 128), F32),
            pltpu.VMEM((4, 32, 256), BF),
            pltpu.VMEM((6, 32, 256), BF),
            pltpu.VMEM((2, ROWS, 128), F32),
            pltpu.VMEM((ROWS, 128), BF),
            pltpu.VMEM((ROWS, 128), BF),
            pltpu.VMEM((ROWS, 128), BF),
            pltpu.VMEM((16, PIECE, 128), BF),
            pltpu.VMEM((8, PIECE, 128), BF),
            pltpu.VMEM((2, ROWS, 128), BF),
            dma((24,)),
            dma((3, 2, 3)),
            dma((4,)),
        ],
        compiler_params=pltpu.CompilerParams(
            collective_id=0, has_side_effects=True, vmem_limit_bytes=48 * 2**20
        ),
        name="block",
    )(
        taps,
        cycle_weight,
        field,
        cotangent,
        legendre,
        gain,
        mixing,
        filter_weight,
        jnp.asarray(pick, BF),
        jnp.asarray(gain_pick, BF),
        jnp.asarray(wide, BF),
        jnp.asarray(across, BF),
    )


def per_device(
    field,
    cotangent,
    legendre,
    cycle_weight,
    support_tap,
    support_basis,
    support_weight,
    filter_weight,
    spectral_weight,
    spectral_gain,
):
    lat, lon = lax.axis_index("lat"), lax.axis_index("lon")
    spots = lat * 4 - 1 + jnp.arange(6, dtype=jnp.int32)
    inside = (spots >= 0) & (spots < LATITUDES)
    code = support_tap * BASIS_COUNT + support_basis
    reach = jnp.clip(spots, 0, LATITUDES - 1)
    hit = code[reach][:, :, None] == jnp.arange(9 * BASIS_COUNT, dtype=jnp.int32)
    hit = hit & inside[:, None, None]
    taps = jnp.sum(jnp.where(hit, support_weight[reach][:, :, None], 0.0), axis=1)
    taps = taps.astype(BF).astype(F32)
    table = legendre.reshape(16, 3, 128, 4).transpose(0, 1, 3, 2).reshape(16, 12, 128)
    table = jnp.pad(table, ((0, 0), (0, 4), (0, 0)))
    at = jnp.arange(4, dtype=jnp.int32) == lon
    gain = jnp.where(at[None, :, None], spectral_gain[:, None, :], 0).reshape(6, 2, 128)
    gain = jnp.pad(gain.transpose(1, 0, 2).reshape(12, 128), ((0, 4), (0, 0)))
    output, grad_field, grad_filter, grad_spectral = block_call(
        taps,
        cycle_weight,
        field,
        cotangent,
        table,
        gain,
        spectral_weight,
        filter_weight.reshape(1024, 256),
    )
    return (output, grad_field, grad_filter.reshape(4, 256, 256), grad_spectral)


def solution(mesh):
    placed = (
        P("lat", "lon", None),
        P("lat", "lon", None),
        P(None, None, "lat"),
        P("lat"),
        P(),
        P(),
        P(),
        P(),
        P(),
        P("lat", "lon"),
    )
    return jax.shard_map(
        per_device,
        mesh=mesh,
        in_specs=placed,
        out_specs=(P("lat", "lon", None), P("lat", "lon", None), P(), P(None, "lon")),
        check_vma=False,
    )
```

```python
import math

import jax
import jax.numpy as jnp
import numpy as np
from jax import lax
from jax.experimental import pallas as pl
from jax.experimental.pallas import tpu as pltpu
from jax.sharding import PartitionSpec as P

LATITUDES = 256
LONGITUDES = 768
DEGREES = 384
ORDERS = 16
BASIS_COUNT = 4
LAT = 64
LON = 4
WIDTH = LONGITUDES // LON
WIDE = WIDTH + 32
ROWS = 1280
PIECE = 80
MESH = pl.DeviceIdType.MESH
BF = jnp.bfloat16
F32 = jnp.float32


def trig_tables():
    longitude = np.arange(LONGITUDES)
    order = np.arange(ORDERS)
    angle = (longitude[:, None] * order[None, :] % LONGITUDES) * (2.0 * math.pi / LONGITUDES)
    table = np.stack([np.cos(angle), np.sin(angle)], axis=2).reshape(LONGITUDES, 2 * ORDERS)
    both = np.stack([table * LONGITUDES ** (-0.5), table * (2 * ORDERS) ** (-0.5)])
    both = both.astype(np.float32)
    where = np.arange(LON)[:, None] * WIDTH + np.arange(-16, WIDTH + 16)[None, :]
    wide = both[:, where % LONGITUDES].transpose(1, 0, 2, 3)
    across = wide[:, :, 16 : 16 + WIDTH].transpose(0, 1, 3, 2)
    return wide, across


def whole_wait(ref, sem):
    pltpu.make_async_copy(ref, ref, sem).wait()


def unpack_constants():
    pick = np.zeros((3, 128, 256), np.float32)
    gain_pick = np.zeros((2, 48, 256), np.float32)
    for dev in range(8):
        for block in range(3):
            for group in range(4):
                for cycle in range(4):
                    pick[block, dev * 16 + group * 4 + cycle, dev * 32 + block * 4 + cycle] = 1.0
        for half in range(2):
            for degree in range(6):
                gain_pick[half, dev * 6 + degree, dev * 32 + 16 + half * 6 + degree] = 1.0
    return pick, gain_pick


def block_kernel(
    cycle_weight_ref,
    field_ref,
    cot_ref,
    legendre_ref,
    gain_ref,
    mixing_hbm,
    filter_hbm,
    pick_hbm,
    gain_pick_hbm,
    wide_hbm,
    across_hbm,
    support_tap_hbm,
    support_basis_hbm,
    support_weight_hbm,
    out_ref,
    grad_ref,
    sums_ref,
    mixing_ref,
    filter_ref,
    pick_ref,
    gain_pick_ref,
    wide_ref,
    across_ref,
    support_tap_ref,
    support_basis_ref,
    support_weight_ref,
    field_wide,
    cot_wide,
    grad_wide,
    band,
    band_back,
    filtered,
    filtered_t,
    hidden,
    grad_own,
    partial,
    part_buf,
    gain_wide,
    gain_src,
    gain_buf,
    table_src,
    table_buf,
    mode_buf,
    rep,
    rep_t,
    gain_all,
    spec,
    scaled_s,
    mixed,
    back_src,
    cycle_buf,
    cycle_wide,
    near_cycles,
    terms,
    core_src,
    core_buf,
    plane_src,
    plane_buf,
    z_buf,
    sem,
    lon_sem,
    near_sem,
    load_sem,
    sum_sem,
):
    a = lax.axis_index("lat")
    b = lax.axis_index("lon")
    x = lax.rem(a, 4)
    y_lo = lax.rem(lax.div(a, 4), 2)
    z = lax.div(a, 8)
    core = lax.rem(b, 2)
    y_hi = lax.div(b, 2)
    place = (y_hi * 2 + y_lo) * 4 + x
    other_core = y_hi * 2 + 1 - core
    north, south = lax.rem(a + LAT - 1, LAT), lax.rem(a + 1, LAT)
    west, east = lax.rem(b + LON - 1, LON), lax.rem(b + 1, LON)
    slot = z * 4 + x
    barrier = pltpu.get_barrier_semaphore()

    def plane_peer(g):
        py, px = lax.div(g, 4), lax.rem(g, 4)
        return (z * 8 + lax.rem(py, 2) * 4 + px, lax.div(py, 2) * 2 + core)

    def z_peer(g):
        return (g * 8 + y_lo * 4 + x, b)

    def greet(device):
        pl.semaphore_signal(barrier, inc=1, device_id=device, device_id_type=MESH)

    def row_peer(index):
        return lax.div(index, 4) * 8 + y_lo * 4 + lax.rem(index, 4)

    def greet_row(d, carry):
        greet((row_peer(lax.rem(slot + d, 32)), b))
        return carry

    def greet_source(d, carry):
        greet((lax.div(d, 4) * 8 + y_lo * 4 + b, lax.rem(d, 4)))
        return carry

    def greet_plane(d, carry):
        greet(plane_peer(lax.rem(place + d, 16)))
        return carry

    for d in range(1, LON):
        greet((a, lax.rem(b + d, LON)))
    for d in range(LON):
        greet((z * 8 + (1 - y_lo) * 4 + x, d))
    for lat in (north, south):
        greet((lat, b))
        for lon in (west, east):
            greet((lat, lon))
    lax.fori_loop(1, 16, greet_plane, 0)
    lax.fori_loop(1, 32, greet_row, 0)

    @pl.when(b == x)
    def greet_sources_but_me():
        def one(d, carry):
            index = lax.rem(z * 4 + b + d, 32)
            return greet_source(index, carry)

        lax.fori_loop(1, 32, one, 0)

    @pl.when(b != x)
    def greet_sources():
        lax.fori_loop(0, 32, greet_source, 0)

    def send(src, dst, send_sem, recv_sem, device):
        copy = pltpu.make_async_remote_copy(
            src_ref=src,
            dst_ref=dst,
            send_sem=send_sem,
            recv_sem=recv_sem,
            device_id=device,
            device_id_type=MESH,
        )
        copy.start()
        return copy

    inner, middle = pl.ds(1, 4), pl.ds(16, WIDTH)
    loads = [
        pltpu.make_async_copy(src, dst, load_sem.at[n])
        for n, (src, dst) in enumerate(
            (
                (field_ref, field_wide.at[inner, middle, :]),
                (cot_ref, cot_wide.at[inner, middle, :]),
                (across_hbm.at[b], across_ref),
                (support_tap_hbm, support_tap_ref),
                (support_basis_hbm, support_basis_ref),
                (support_weight_hbm, support_weight_ref),
                (filter_hbm, filter_ref),
                (pick_hbm, pick_ref),
                (gain_pick_hbm, gain_pick_ref),
                (mixing_hbm, mixing_ref),
                (wide_hbm.at[b], wide_ref),
            )
        )
    ]
    for load in loads:
        load.start()

    lane = lax.broadcasted_iota(jnp.int32, (6, 128), 1)
    own_gain = gain_ref[...].astype(F32)
    own_gain = jnp.concatenate([own_gain, own_gain], axis=1)
    own_gain = jnp.where(lax.div(lane, 64) == core, own_gain, 0.0)
    gain_wide[...] = jnp.zeros((16, 128), F32)
    for h in range(2):
        gain_wide[h * 6 : h * 6 + 6, :] = jnp.where(y_hi == h, own_gain, 0.0)
    gain_src[...] = gain_wide[...].astype(BF)

    def pack_partial(which, table, rows, scale):
        for i in range(4):
            sums = jnp.dot(across_ref[table], rows(i), preferred_element_type=F32)
            if scale:
                sums = sums * cycle_weight_ref[i]
            for h in range(2):
                partial[which, pl.ds(h * 4 + i, 32, stride=8), :] = sums[:, h * 128 : h * 128 + 128]

    def eight(index):
        return pl.ds(pl.multiple_of(index * 8, 8), 8)

    def send_partial(which, send_sem, recv_sem, own_sem):
        def remote(tr):
            src, dst = partial.at[which, eight(tr), :], part_buf.at[which, z, b]
            send(src, dst, send_sem, recv_sem, (row_peer(tr), x))

        def one(d, carry):
            remote(lax.rem(slot + d, 32))
            return carry

        @pl.when(b == x)
        def to_me():
            pltpu.make_async_copy(
                partial.at[which, eight(slot), :], part_buf.at[which, z, b], own_sem
            ).start()

        @pl.when(b != x)
        def to_peer():
            remote(slot)

        lax.fori_loop(1, 32, one, 0)

    def partial_size(which, count):
        return partial.at[which, pl.ds(0, 8 * count), :]

    def wait_partial(which, send_or_recv_sem, own_sem):
        @pl.when(b == x)
        def with_mine():
            if own_sem is not None:
                whole_wait(partial_size(which, 1), own_sem)
            whole_wait(partial_size(which, 31), send_or_recv_sem)

        @pl.when(b != x)
        def without():
            whole_wait(partial_size(which, 32), send_or_recv_sem)

    loads[0].wait()
    pl.semaphore_wait(barrier, 3 + 4 + 6 + 15 + 31 + 32 - jnp.where(b == x, 1, 0))

    def send_rims(wide, side_send, side_recv, lat_send, lat_recv):
        last, first = pl.ds(WIDTH, 16), pl.ds(16, 16)
        left, right = pl.ds(0, 16), pl.ds(WIDTH + 16, 16)
        top, bottom = wide.at[1], wide.at[4]
        send(wide.at[inner, last], wide.at[inner, left], side_send, side_recv, (a, east))
        send(wide.at[inner, first], wide.at[inner, right], side_send, side_recv, (a, west))
        send(bottom.at[middle], wide.at[0, middle], lat_send, lat_recv, (south, b))
        send(top.at[middle], wide.at[5, middle], lat_send, lat_recv, (north, b))
        send(bottom.at[last], wide.at[0, left], lat_send, lat_recv, (south, east))
        send(bottom.at[first], wide.at[0, right], lat_send, lat_recv, (south, west))
        send(top.at[last], wide.at[5, left], lat_send, lat_recv, (north, east))
        send(top.at[first], wide.at[5, right], lat_send, lat_recv, (north, west))

    def side_size(wide):
        return wide.at[pl.ds(0, 4), pl.ds(0, 32), :]

    def lat_size(wide):
        return wide.at[pl.ds(0, 2), :, :]

    def to_lon(src, buf, kind):
        return [
            send(
                src,
                buf.at[d - 1],
                lon_sem.at[kind, 0, d - 1],
                lon_sem.at[kind, 1, d - 1],
                (a, lax.rem(b + d, LON)),
            )
            for d in range(1, LON)
        ]

    send_rims(field_wide, sem.at[0], sem.at[1], sem.at[24], sem.at[25])
    gain_copies = to_lon(gain_src, gain_buf, 0)

    for copy in gain_copies:
        copy.wait()
    gain_row = gain_src[...].astype(F32)
    for d in range(LON - 1):
        gain_row = gain_row + gain_buf[d].astype(F32)
    gain_row = gain_row.astype(BF)
    for t in range(ORDERS):
        table_src[t, 0:16, :] = legendre_ref[t]
        table_src[t, 16:32, :] = gain_row

    def send_table(d, carry):
        to_z, to_x = lax.rem(z + d, 8), lax.rem(b + 1, 4)
        src = table_src.at[to_z * 2 + lax.div(to_x, 2)]
        dst = table_buf.at[z, y_lo, lax.div(x, 2), lax.rem(x, 2)]
        send(src, dst, sem.at[2], sem.at[3], (to_z * 8 + y_lo * 4 + to_x, x))
        return carry

    lax.fori_loop(0, 8, send_table, 0)
    loads[1].wait()
    loads[2].wait()
    pack_partial(1, 1, lambda i: cot_wide[i + 1, 16 : 16 + WIDTH, :], False)
    send_partial(1, sem.at[26], sem.at[27], sem.at[28])

    for load in loads[3:6]:
        load.wait()
    entry = lax.broadcasted_iota(jnp.int32, (18, 128), 1)
    place_of = lax.broadcasted_iota(jnp.int32, (18, LATITUDES), 1)
    code = (support_tap_ref[...] * BASIS_COUNT + support_basis_ref[...]).astype(F32)
    columns = []
    for r in range(6):
        here = place_of == a * 4 + r - 1
        own_code = jnp.sum(jnp.where(here, code, 0.0), axis=1, keepdims=True)
        own_weight = jnp.sum(
            jnp.where(here, support_weight_ref[...], 0.0), axis=1, keepdims=True
        )
        kept = jnp.where(own_code == entry.astype(F32), own_weight, 0.0)
        columns.append(jnp.sum(kept, axis=0, keepdims=True).astype(BF).astype(F32))

    diagonal = lax.broadcasted_iota(jnp.int32, (96, 128), 1)
    diagonal = diagonal - lax.broadcasted_iota(jnp.int32, (96, 128), 0) - 15
    inside_north = jnp.where(a == 0, 0.0, 1.0)
    inside_south = jnp.where(a == LAT - 1, 0.0, 1.0)

    def make_band(dst, i, adjoint):
        for p in range(3):
            for k in range(BASIS_COUNT):
                block = jnp.zeros((96, 128), F32)
                for q in range(3):
                    if adjoint:
                        column, at = columns[i + p], (8 - 3 * p - q) * BASIS_COUNT + k
                    else:
                        column, at = columns[i + 1], (3 * p + q) * BASIS_COUNT + k
                    value = column[:, at : at + 1]
                    if not adjoint:
                        if i == 0 and p == 0:
                            value = value * inside_north
                        if i == 3 and p == 2:
                            value = value * inside_south
                    block = jnp.where(diagonal == q, value, block)
                dst[i, k * 96 : k * 96 + 96, p * 128 : p * 128 + 128] = block.astype(BF)

    for i in range(4):
        make_band(band, i, False)

    def stencil(src, bands, i, block):
        near = jnp.concatenate([src[i + p, block * 96 : block * 96 + 128, :] for p in range(3)])
        return jnp.dot(bands[i], near, preferred_element_type=F32).astype(BF)

    whole_wait(table_buf.at[:, 0, 0, 0], sem.at[3])
    column_block = table_buf.at[:, y_lo, y_hi, core]
    for d in range(1, 4):
        y = lax.rem(y_hi * 2 + y_lo + d, 4)
        peer = (z * 8 + lax.rem(y, 2) * 4 + x, lax.div(y, 2) * 2 + core)
        send(column_block, column_block, sem.at[31], sem.at[32], peer)

    loads[6].wait()
    whole_wait(side_size(field_wide), sem.at[1])

    def filter_cycle(i):
        for block in range(2):
            sums = stencil(field_wide, band, i, block)
            first = i * WIDTH + block * 96
            for k in range(BASIS_COUNT):
                filtered[first : first + 96, k * 256 : k * 256 + 256] = sums[k * 96 : k * 96 + 96]
        own = slice(i * WIDTH, i * WIDTH + WIDTH)
        mix = jnp.dot(filtered[own, :], filter_ref[...], preferred_element_type=F32)
        own_field = field_wide[i + 1, 16 : 16 + WIDTH, :].astype(F32)
        hidden[i] = (own_field + mix).astype(BF)

    filter_cycle(1)
    filter_cycle(2)

    whole_wait(lat_size(field_wide), sem.at[25])
    filter_cycle(0)
    filter_cycle(3)
    pack_partial(0, 0, lambda i: hidden[i], True)
    send_partial(0, sem.at[7], sem.at[33], sem.at[9])

    whole_wait(table_buf.at[pl.ds(0, 6), 0], sem.at[32])
    core_table = table_buf.at[:, :, :, core]
    table_copy = send(core_table, core_table, sem.at[34], sem.at[35], (a, other_core))

    for k in range(BASIS_COUNT):
        for pair in range(2):
            rows = filtered[pair * 384 : pair * 384 + 384, k * 256 : k * 256 + 256]
            filtered_t[k * 256 : k * 256 + 256, pair * 384 : pair * 384 + 384] = rows.T
    for i in range(4):
        make_band(band_back, i, True)

    wait_partial(1, sem.at[27], sem.at[28])
    wait_partial(0, sem.at[33], sem.at[9])
    totals = []
    for which in range(2):
        total = part_buf[which, :, 0]
        for d in range(1, LON):
            total = total + part_buf[which, :, d]
        totals.append(total)
    mode_buf[:, y_lo, b] = jnp.concatenate(totals, axis=1).astype(BF)
    own_modes = mode_buf.at[:, y_lo, b]
    for d in range(1, 8):
        g = lax.rem(y_lo * 4 + b + d, 8)
        peer = (z * 8 + lax.div(g, 4) * 4 + x, lax.rem(g, 4))
        send(own_modes, own_modes, sem.at[36], sem.at[8], peer)

    def tile(index):
        return pl.ds(pl.multiple_of(index * 16, 16), 16)

    send_rims(cot_wide, sem.at[5], sem.at[6], sem.at[29], sem.at[30])

    for load in loads[7:]:
        load.wait()
    table_copy.wait()
    for chunk in range(8):
        packed = table_buf[chunk].reshape(256, 128)
        for block in range(3):
            rows = jnp.dot(pick_ref[block], packed, preferred_element_type=F32)
            lanes = slice(block * 128, block * 128 + 128)
            rep[chunk, :, :, lanes] = rows.astype(BF).reshape(2, 64, 128)
            rep_t[lanes, chunk * 128 : chunk * 128 + 128] = rows.T.astype(BF)
        for side in range(2):
            rows = jnp.dot(gain_pick_ref[side], packed, preferred_element_type=F32)
            gain_all[chunk * 48 : chunk * 48 + 48, side * 128 : side * 128 + 128] = rows

    whole_wait(mode_buf.at[pl.ds(0, 7)], sem.at[8])
    group = lax.rem(lax.div(lax.broadcasted_iota(jnp.int32, (1024, 128), 0), 4), 4)
    modes = mode_buf[...].reshape(1024, 128).astype(F32)
    for g in range(4):
        kept = jnp.where(group == g, modes, 0.0).astype(BF)
        spec[:, g * 128 : g * 128 + 128] = jnp.dot(
            rep_t[...], kept, preferred_element_type=F32
        ).astype(BF)
    gains = gain_all[...]
    mixed[:, 0:256] = (
        gains * jnp.dot(spec[:, 0:256], mixing_ref[...], preferred_element_type=F32)
    ).astype(BF)
    scaled_s[...] = (gains * spec[:, 256:512].astype(F32)).astype(BF)
    mixed[:, 256:512] = lax.dot_general(
        scaled_s[...], mixing_ref[...], (((1,), (1,)), ((), ())), preferred_element_type=F32
    ).astype(BF)
    group = lax.rem(lax.div(lax.broadcasted_iota(jnp.int32, (512, 128), 0), 4), 4)
    rows = rep[:, y_lo].reshape(512, DEGREES)
    packed = jnp.zeros((512, 128), F32)
    for g in range(4):
        sums = jnp.dot(rows, mixed[:, g * 128 : g * 128 + 128], preferred_element_type=F32)
        packed = jnp.where(group == g, sums, packed)
    back_src[...] = packed.astype(BF)

    def send_back(d, carry):
        to = lax.rem(slot + d, 32)
        src = back_src.at[tile(to), :]
        dst = cycle_buf.at[tile(slot), :]
        send(src, dst, sem.at[10], sem.at[11], (row_peer(to), b))
        return carry

    lax.fori_loop(1, 32, send_back, 0)
    own_back = pltpu.make_async_copy(
        back_src.at[tile(slot), :], cycle_buf.at[tile(slot), :], sem.at[12]
    )
    own_back.start()

    degrees = pl.ds(pl.multiple_of((y_lo * 4 + b) * 48, 16), 48)
    term = lax.dot_general(
        spec[degrees, 0:256],
        scaled_s[degrees, :],
        (((0,), (0,)), ((), ())),
        preferred_element_type=F32,
    )
    for h in range(2):
        terms[h, 1024:1280, :] = term[:, h * 128 : h * 128 + 128]

    parts = ((1024, 256), (0, 512), (512, 512))

    def part_rows(n):
        return pl.ds(parts[n][0], parts[n][1])

    def piece(n, g):
        size = parts[n][1] // 16
        return pl.ds(pl.multiple_of(parts[n][0] + g * size, 16), size)

    def plane_slots(n, count):
        size = parts[n][1] // 16
        return pl.ds(parts[n][0] // 16 * 15, count * size)

    def core_send(n):
        rows = part_rows(n)
        core_src[rows, :] = terms[1 - core, rows, :].astype(BF)
        return send(
            core_src.at[rows],
            core_buf.at[rows],
            sum_sem.at[n, 0],
            sum_sem.at[n, 1],
            (a, other_core),
        )

    def plane_send(n, core_copy):
        rows, size = part_rows(n), parts[n][1] // 16
        core_copy.wait()
        plane_src[rows, :] = (terms[core, rows, :] + core_buf[rows, :].astype(F32)).astype(BF)

        def one(d, carry):
            g = lax.rem(place + d, 16)
            slot_rows = pl.ds(
                pl.multiple_of(parts[n][0] // 16 * 15 + (d - 1) * size, 16), size
            )
            send(
                plane_src.at[piece(n, g)],
                plane_buf.at[slot_rows],
                sum_sem.at[n, 2],
                sum_sem.at[n, 3],
                plane_peer(g),
            )
            return carry

        lax.fori_loop(1, 16, one, 0)

    def z_rows(n):
        return pl.ds(parts[n][0] // 16, parts[n][1] // 16)

    def z_send(n):
        size = parts[n][1] // 16
        whole_wait(plane_buf.at[plane_slots(n, 15)], sum_sem.at[n, 3])
        total = plane_src[piece(n, place), :].astype(F32)
        for d in range(15):
            first = parts[n][0] // 16 * 15 + d * size
            total = total + plane_buf[first : first + size, :].astype(F32)
        z_buf[z, z_rows(n), :] = total.astype(BF)
        mine = z_buf.at[z, z_rows(n)]

        def one(d, carry):
            send(mine, mine, sum_sem.at[n, 4], sum_sem.at[n, 5], z_peer(lax.rem(z + d, 8)))
            return carry

        lax.fori_loop(1, 8, one, 0)

    def z_size(n):
        return z_buf.at[pl.ds(0, 7), z_rows(n)]

    def gather_send(n):
        whole_wait(z_size(n), sum_sem.at[n, 5])
        total = z_buf[0, z_rows(n), :].astype(F32)
        for g in range(1, 8):
            total = total + z_buf[g, z_rows(n), :].astype(F32)
        sums_ref[core, piece(n, place), :] = total.astype(BF)
        mine = sums_ref.at[core, piece(n, place)]

        def one(d, carry):
            send(
                mine,
                mine,
                sum_sem.at[n, 6],
                sum_sem.at[n, 7],
                plane_peer(lax.rem(place + d, 16)),
            )
            return carry

        lax.fori_loop(1, 16, one, 0)

    def last_send(n):
        whole_wait(plane_buf.at[plane_slots(n, 15)], sum_sem.at[n, 7])
        half_sums = sums_ref.at[core, part_rows(n)]
        return send(half_sums, half_sums, sum_sem.at[n, 8], sum_sem.at[n, 9], (a, other_core))

    spectral_copy = core_send(0)
    plane_send(0, spectral_copy)

    own_back.wait()
    whole_wait(cycle_buf.at[pl.ds(0, 16 * 31), :], sem.at[11])
    cycle_wide[...] = cycle_buf[...].astype(F32)

    def cycle_rows(which, i):
        return jnp.concatenate(
            [cycle_wide[pl.ds(which * 8 + h * 4 + i, 32, stride=16), :] for h in range(2)], axis=1
        )

    for i in (0, 3, 1, 2):
        near_cycles[i + 1] = (cycle_rows(1, i) * cycle_weight_ref[i]).astype(BF)
    near_copies = [
        send(near_cycles.at[1], near_cycles.at[5], near_sem.at[0], near_sem.at[1], (north, b)),
        send(near_cycles.at[4], near_cycles.at[0], near_sem.at[2], near_sem.at[3], (south, b)),
    ]

    def make_grad(r):
        spatial = jnp.dot(wide_ref[0], near_cycles[r], preferred_element_type=F32).astype(BF)
        return (cot_wide[r].astype(F32) + spatial.astype(F32)).astype(BF)

    whole_wait(side_size(cot_wide), sem.at[6])
    whole_wait(lat_size(cot_wide), sem.at[30])
    for i in range(4):
        grad = make_grad(i + 1)
        grad_wide[i + 1] = grad
        grad_own[i * WIDTH : i * WIDTH + WIDTH, :] = grad[16 : 16 + WIDTH]
    def filter_terms(k):
        own = slice(k * 256, k * 256 + 256)
        term = jnp.dot(filtered_t[own, :], grad_own[...], preferred_element_type=F32)
        for h in range(2):
            terms[h, own, :] = term[:, h * 128 : h * 128 + 128]

    filter_terms(0)
    filter_terms(1)
    first_copy = core_send(1)
    filter_terms(2)
    filter_terms(3)
    second_copy = core_send(2)
    z_send(0)
    plane_send(1, first_copy)

    def finish_output(i):
        fore = cycle_rows(0, i).astype(BF)
        spatial = jnp.dot(wide_ref[1, 16 : 16 + WIDTH, :], fore, preferred_element_type=F32)
        out_ref[i] = (hidden[i].astype(F32) + spatial.astype(BF).astype(F32)).astype(BF)

    finish_output(0)
    plane_send(2, second_copy)
    finish_output(1)
    gather_send(0)
    finish_output(2)
    finish_output(3)
    for copy in near_copies:
        copy.wait()
    for r in (0, 5):
        grad_wide[r] = make_grad(r)

    def field_grad(i):
        total = grad_own[i * WIDTH : i * WIDTH + WIDTH, :].astype(F32)
        done = []
        for block in range(2):
            sums = stencil(grad_wide, band_back, i, block)
            part = total[block * 96 : block * 96 + 96]
            for k in range(BASIS_COUNT):
                part = part + lax.dot_general(
                    sums[k * 96 : k * 96 + 96],
                    filter_ref[k * 256 : k * 256 + 256, :],
                    (((1,), (1,)), ((), ())),
                    preferred_element_type=F32,
                )
            done.append(part)
        grad_ref[i] = jnp.concatenate(done).astype(BF)

    z_send(1)
    field_grad(0)
    z_send(2)
    field_grad(1)
    last_copies = [last_send(0)]
    gather_send(1)
    field_grad(2)
    gather_send(2)
    field_grad(3)
    last_copies.append(last_send(1))
    last_copies.append(last_send(2))

    whole_wait(side_size(field_wide), sem.at[0])
    whole_wait(lat_size(field_wide), sem.at[24])
    whole_wait(side_size(cot_wide), sem.at[5])
    whole_wait(lat_size(cot_wide), sem.at[29])
    wait_partial(1, sem.at[26], None)
    wait_partial(0, sem.at[7], None)
    whole_wait(table_buf.at[:, 0, 0, 0], sem.at[2])
    whole_wait(table_buf.at[pl.ds(0, 6), 0], sem.at[31])
    whole_wait(mode_buf.at[pl.ds(0, 7)], sem.at[36])
    whole_wait(cycle_buf.at[pl.ds(0, 16 * 31), :], sem.at[10])
    for n in range(3):
        whole_wait(plane_buf.at[plane_slots(n, 15)], sum_sem.at[n, 2])
        whole_wait(z_size(n), sum_sem.at[n, 4])
        whole_wait(plane_buf.at[plane_slots(n, 15)], sum_sem.at[n, 6])
    for copy in last_copies:
        copy.wait()


def finish_kernel(sums_hbm, out_hbm, grad_hbm, out_ref, grad_ref, filter_ref, spectral_ref, *scratch):
    sums_ref, filter_vmem, spectral_vmem, out_vmem, grad_vmem, sem = scratch
    b = lax.axis_index("lon")
    copies = [
        pltpu.make_async_copy(sums_hbm, sums_ref, sem.at[0]),
        pltpu.make_async_copy(out_hbm, out_vmem, sem.at[1]),
        pltpu.make_async_copy(grad_hbm, grad_vmem, sem.at[2]),
    ]
    for copy in copies:
        copy.start()
    copies[0].wait()
    grid_scale = (LATITUDES * LONGITUDES) ** (-0.5)
    for k in range(BASIS_COUNT):
        for h in range(2):
            rows, lanes = slice(k * 256, k * 256 + 256), slice(h * 128, h * 128 + 128)
            filter_vmem[rows, lanes] = sums_ref[h, rows, :].astype(F32) * grid_scale
        rows = pl.ds(k * 256, 256)
        copies.append(
            pltpu.make_async_copy(filter_vmem.at[rows], filter_ref.at[rows], sem.at[3 + k])
        )
        copies[-1].start()
    columns = sums_ref[lax.div(b, 2), 1024:1280, :].astype(F32)
    columns = columns * (2 * ORDERS * DEGREES) ** (-0.5)
    spectral_vmem[...] = jnp.where(
        lax.rem(b, 2) == 0, columns[:, 0:64], columns[:, 64:128]
    ).T
    copies.append(pltpu.make_async_copy(spectral_vmem, spectral_ref, sem.at[7]))
    copies[-1].start()
    for n, (staged, target) in enumerate(((out_vmem, out_ref), (grad_vmem, grad_ref))):
        copies[1 + n].wait()
        copies.append(pltpu.make_async_copy(staged, target, sem.at[8 + n]))
        copies[-1].start()
    for copy in copies[3:]:
        copy.wait()


def finish_call(sums, out, grad):
    anywhere = pl.BlockSpec(memory_space=pl.ANY)
    return pl.pallas_call(
        finish_kernel,
        out_shape=(
            jax.ShapeDtypeStruct((4, WIDTH, 256), BF),
            jax.ShapeDtypeStruct((4, WIDTH, 256), BF),
            jax.ShapeDtypeStruct((1024, 256), F32),
            jax.ShapeDtypeStruct((64, 256), F32),
        ),
        in_specs=[anywhere] * 3,
        out_specs=(anywhere,) * 4,
        scratch_shapes=[
            pltpu.VMEM((2, ROWS, 128), BF),
            pltpu.VMEM((1024, 256), F32),
            pltpu.VMEM((64, 256), F32),
            pltpu.VMEM((4, WIDTH, 256), BF),
            pltpu.VMEM((4, WIDTH, 256), BF),
            pltpu.SemaphoreType.DMA((10,)),
        ],
        compiler_params=pltpu.CompilerParams(vmem_limit_bytes=60 * 2**20),
        name="finish",
    )(sums, out, grad)


def block_call(cycle_weight, field, cotangent, legendre, gain, mixing, filter_weight, support):
    pick, gain_pick = unpack_constants()
    wide, across = trig_tables()
    vmem = pl.BlockSpec(memory_space=pltpu.VMEM)
    smem = pl.BlockSpec(memory_space=pltpu.SMEM)
    anywhere = pl.BlockSpec(memory_space=pl.ANY)
    dma = pltpu.SemaphoreType.DMA
    return pl.pallas_call(
        block_kernel,
        out_shape=(
            jax.ShapeDtypeStruct((4, WIDTH, 256), BF),
            jax.ShapeDtypeStruct((4, WIDTH, 256), BF),
            jax.ShapeDtypeStruct((2, ROWS, 128), BF),
        ),
        in_specs=[smem, anywhere, anywhere, vmem, vmem] + [anywhere] * 9,
        out_specs=(vmem,) * 3,
        scratch_shapes=[
            pltpu.VMEM((256, 256), BF),
            pltpu.VMEM((1024, 256), BF),
            pltpu.VMEM((3, 128, 256), BF),
            pltpu.VMEM((2, 48, 256), BF),
            pltpu.VMEM((2, WIDE, 32), BF),
            pltpu.VMEM((2, 32, WIDTH), BF),
            pltpu.VMEM((18, LATITUDES), jnp.int32),
            pltpu.VMEM((18, LATITUDES), jnp.int32),
            pltpu.VMEM((18, LATITUDES), F32),
            pltpu.VMEM((6, WIDE, 256), BF),
            pltpu.VMEM((6, WIDE, 256), BF),
            pltpu.VMEM((6, WIDE, 256), BF),
            pltpu.VMEM((4, 384, 384), BF),
            pltpu.VMEM((4, 384, 384), BF),
            pltpu.VMEM((768, 1024), BF),
            pltpu.VMEM((1024, 768), BF),
            pltpu.VMEM((4, WIDTH, 256), BF),
            pltpu.VMEM((768, 256), BF),
            pltpu.VMEM((2, 256, 128), F32),
            pltpu.VMEM((2, 8, LON, 8, 128), F32),
            pltpu.VMEM((16, 128), F32),
            pltpu.VMEM((16, 128), BF),
            pltpu.VMEM((3, 16, 128), BF),
            pltpu.VMEM((16, 32, 128), BF),
            pltpu.VMEM((8, 2, 2, 2, 32, 128), BF),
            pltpu.VMEM((8, 2, 4, 16, 128), BF),
            pltpu.VMEM((8, 2, 64, DEGREES), BF),
            pltpu.VMEM((DEGREES, 1024), BF),
            pltpu.VMEM((DEGREES, 256), F32),
            pltpu.VMEM((DEGREES, 512), BF),
            pltpu.VMEM((DEGREES, 256), BF),
            pltpu.VMEM((DEGREES, 512), BF),
            pltpu.VMEM((512, 128), BF),
            pltpu.VMEM((512, 128), BF),
            pltpu.VMEM((512, 128), F32),
            pltpu.VMEM((6, 32, 256), BF),
            pltpu.VMEM((2, ROWS, 128), F32),
            pltpu.VMEM((ROWS, 128), BF),
            pltpu.VMEM((ROWS, 128), BF),
            pltpu.VMEM((ROWS, 128), BF),
            pltpu.VMEM((15 * PIECE, 128), BF),
            pltpu.VMEM((8, PIECE, 128), BF),
            dma((37,)),
            dma((1, 2, 3)),
            dma((4,)),
            dma((11,)),
            dma((3, 10)),
        ],
        compiler_params=pltpu.CompilerParams(
            collective_id=0, has_side_effects=True, vmem_limit_bytes=60 * 2**20
        ),
        name="block",
    )(
        cycle_weight,
        field,
        cotangent,
        legendre,
        gain,
        mixing,
        filter_weight,
        jnp.asarray(pick, BF),
        jnp.asarray(gain_pick, BF),
        jnp.asarray(wide, BF),
        jnp.asarray(across, BF),
        *support,
    )


def per_device(
    field,
    cotangent,
    legendre,
    cycle_weight,
    support_tap,
    support_basis,
    support_weight,
    filter_weight,
    spectral_weight,
    spectral_gain,
):
    table = legendre.reshape(16, 3, 128, 4).transpose(0, 1, 3, 2).reshape(16, 12, 128)
    table = jnp.pad(table, ((0, 0), (0, 4), (0, 0)))
    output, grad_field, sums = block_call(
        cycle_weight,
        field,
        cotangent,
        table,
        spectral_gain,
        spectral_weight,
        filter_weight.reshape(1024, 256),
        (support_tap.T, support_basis.T, support_weight.T),
    )
    output, grad_field, grad_filter, grad_spectral = finish_call(sums, output, grad_field)
    return (output, grad_field, grad_filter.reshape(4, 256, 256), grad_spectral.T)


def solution(mesh):
    placed = (
        P("lat", "lon", None),
        P("lat", "lon", None),
        P(None, None, "lat"),
        P("lat"),
        P(),
        P(),
        P(),
        P(),
        P(),
        P("lat", "lon"),
    )
    return jax.shard_map(
        per_device,
        mesh=mesh,
        in_specs=placed,
        out_specs=(P("lat", "lon", None), P("lat", "lon", None), P(), P(None, "lon")),
        check_vma=False,
    )
```

```python
import math

import jax
import jax.numpy as jnp
import numpy as np
from jax import lax
from jax.experimental import pallas as pl
from jax.experimental.pallas import tpu as pltpu
from jax.sharding import PartitionSpec as P

LATITUDES = 256
LONGITUDES = 768
DEGREES = 384
ORDERS = 16
BASIS_COUNT = 4
LAT = 64
LON = 4
WIDTH = LONGITUDES // LON
WIDE = WIDTH + 32
ROWS = 1280
PIECE = 80
MESH = pl.DeviceIdType.MESH
BF = jnp.bfloat16
F32 = jnp.float32


def trig_tables():
    longitude = np.arange(LONGITUDES)
    order = np.arange(ORDERS)
    angle = (longitude[:, None] * order[None, :] % LONGITUDES) * (2.0 * math.pi / LONGITUDES)
    table = np.stack([np.cos(angle), np.sin(angle)], axis=2).reshape(LONGITUDES, 2 * ORDERS)
    both = np.stack([table * LONGITUDES ** (-0.5), table * (2 * ORDERS) ** (-0.5)])
    both = both.astype(np.float32)
    where = np.arange(LON)[:, None] * WIDTH + np.arange(-16, WIDTH + 16)[None, :]
    wide = both[:, where % LONGITUDES].transpose(1, 0, 2, 3)
    across = wide[:, :, 16 : 16 + WIDTH].transpose(0, 1, 3, 2)
    return wide, across


def whole_wait(ref, sem):
    pltpu.make_async_copy(ref, ref, sem).wait()


def unpack_constants():
    pick = np.zeros((3, 128, 256), np.float32)
    gain_pick = np.zeros((2, 48, 256), np.float32)
    for dev in range(8):
        for block in range(3):
            for group in range(4):
                for cycle in range(4):
                    pick[block, dev * 16 + group * 4 + cycle, dev * 32 + block * 4 + cycle] = 1.0
        for half in range(2):
            for degree in range(6):
                gain_pick[half, dev * 6 + degree, dev * 32 + 16 + half * 6 + degree] = 1.0
    return pick, gain_pick


def block_kernel(
    cycle_weight_ref,
    field_ref,
    cot_ref,
    legendre_ref,
    gain_ref,
    mixing_hbm,
    filter_hbm,
    pick_hbm,
    gain_pick_hbm,
    wide_hbm,
    across_hbm,
    support_tap_hbm,
    support_basis_hbm,
    support_weight_hbm,
    out_ref,
    grad_ref,
    sums_ref,
    mixing_ref,
    filter_ref,
    pick_ref,
    gain_pick_ref,
    wide_ref,
    across_ref,
    support_tap_ref,
    support_basis_ref,
    support_weight_ref,
    field_wide,
    cot_wide,
    grad_wide,
    band,
    band_back,
    filtered,
    filtered_t,
    hidden,
    grad_own,
    partial,
    part_buf,
    gain_wide,
    gain_src,
    gain_buf,
    table_src,
    table_buf,
    mode_buf,
    rep,
    rep_t,
    gain_all,
    spec,
    scaled_s,
    mixed,
    back_src,
    cycle_buf,
    cycle_wide,
    near_cycles,
    terms,
    core_src,
    core_buf,
    plane_src,
    plane_buf,
    z_buf,
    sem,
    lon_sem,
    near_sem,
    load_sem,
    sum_sem,
):
    a = lax.axis_index("lat")
    b = lax.axis_index("lon")
    x = lax.rem(a, 4)
    y_lo = lax.rem(lax.div(a, 4), 2)
    z = lax.div(a, 8)
    core = lax.rem(b, 2)
    y_hi = lax.div(b, 2)
    place = (y_hi * 2 + y_lo) * 4 + x
    other_core = y_hi * 2 + 1 - core
    north, south = lax.rem(a + LAT - 1, LAT), lax.rem(a + 1, LAT)
    west, east = lax.rem(b + LON - 1, LON), lax.rem(b + 1, LON)
    slot = z * 4 + x
    barrier = pltpu.get_barrier_semaphore()

    def plane_peer(g):
        py, px = lax.div(g, 4), lax.rem(g, 4)
        return (z * 8 + lax.rem(py, 2) * 4 + px, lax.div(py, 2) * 2 + core)

    def z_peer(g):
        return (g * 8 + y_lo * 4 + x, b)

    def greet(device):
        pl.semaphore_signal(barrier, inc=1, device_id=device, device_id_type=MESH)

    def row_peer(index):
        return lax.div(index, 4) * 8 + y_lo * 4 + lax.rem(index, 4)

    def greet_row(d, carry):
        greet((row_peer(lax.rem(slot + d, 32)), b))
        return carry

    def greet_source(d, carry):
        greet((lax.div(d, 4) * 8 + y_lo * 4 + b, lax.rem(d, 4)))
        return carry

    def greet_plane(d, carry):
        greet(plane_peer(lax.rem(place + d, 16)))
        return carry

    for d in range(1, LON):
        greet((a, lax.rem(b + d, LON)))
    for d in range(LON):
        greet((z * 8 + (1 - y_lo) * 4 + x, d))
    for lat in (north, south):
        greet((lat, b))
        for lon in (west, east):
            greet((lat, lon))
    lax.fori_loop(1, 16, greet_plane, 0)
    lax.fori_loop(1, 32, greet_row, 0)

    @pl.when(b == x)
    def greet_sources_but_me():
        def one(d, carry):
            index = lax.rem(z * 4 + b + d, 32)
            return greet_source(index, carry)

        lax.fori_loop(1, 32, one, 0)

    @pl.when(b != x)
    def greet_sources():
        lax.fori_loop(0, 32, greet_source, 0)

    def send(src, dst, send_sem, recv_sem, device):
        copy = pltpu.make_async_remote_copy(
            src_ref=src,
            dst_ref=dst,
            send_sem=send_sem,
            recv_sem=recv_sem,
            device_id=device,
            device_id_type=MESH,
        )
        copy.start()
        return copy

    inner, middle = pl.ds(1, 4), pl.ds(16, WIDTH)
    loads = [
        pltpu.make_async_copy(src, dst, load_sem.at[n])
        for n, (src, dst) in enumerate(
            (
                (field_ref, field_wide.at[inner, middle, :]),
                (cot_ref, cot_wide.at[inner, middle, :]),
                (across_hbm.at[b], across_ref),
                (support_tap_hbm, support_tap_ref),
                (support_basis_hbm, support_basis_ref),
                (support_weight_hbm, support_weight_ref),
                (filter_hbm, filter_ref),
                (pick_hbm, pick_ref),
                (gain_pick_hbm, gain_pick_ref),
                (mixing_hbm, mixing_ref),
                (wide_hbm.at[b], wide_ref),
            )
        )
    ]
    for load in loads:
        load.start()

    lane = lax.broadcasted_iota(jnp.int32, (6, 128), 1)
    own_gain = gain_ref[...].astype(F32)
    own_gain = jnp.concatenate([own_gain, own_gain], axis=1)
    own_gain = jnp.where(lax.div(lane, 64) == core, own_gain, 0.0)
    gain_wide[...] = jnp.zeros((16, 128), F32)
    for h in range(2):
        gain_wide[h * 6 : h * 6 + 6, :] = jnp.where(y_hi == h, own_gain, 0.0)
    gain_src[...] = gain_wide[...].astype(BF)

    def pack_partial(which, table, rows, scale):
        for i in range(4):
            sums = jnp.dot(across_ref[table], rows(i), preferred_element_type=F32)
            if scale:
                sums = sums * cycle_weight_ref[i]
            for h in range(2):
                partial[which, pl.ds(h * 4 + i, 32, stride=8), :] = sums[:, h * 128 : h * 128 + 128]

    def eight(index):
        return pl.ds(pl.multiple_of(index * 8, 8), 8)

    def send_partial(which, send_sem, recv_sem, own_sem):
        def remote(tr):
            src, dst = partial.at[which, eight(tr), :], part_buf.at[which, z, b]
            send(src, dst, send_sem, recv_sem, (row_peer(tr), x))

        def one(d, carry):
            remote(lax.rem(slot + d, 32))
            return carry

        @pl.when(b == x)
        def to_me():
            pltpu.make_async_copy(
                partial.at[which, eight(slot), :], part_buf.at[which, z, b], own_sem
            ).start()

        @pl.when(b != x)
        def to_peer():
            remote(slot)

        lax.fori_loop(1, 32, one, 0)

    def partial_size(which, count):
        return partial.at[which, pl.ds(0, 8 * count), :]

    def wait_partial(which, send_or_recv_sem, own_sem):
        @pl.when(b == x)
        def with_mine():
            if own_sem is not None:
                whole_wait(partial_size(which, 1), own_sem)
            whole_wait(partial_size(which, 31), send_or_recv_sem)

        @pl.when(b != x)
        def without():
            whole_wait(partial_size(which, 32), send_or_recv_sem)

    pl.semaphore_wait(barrier, 3 + 4 + 6 + 15 + 31 + 32 - jnp.where(b == x, 1, 0))

    def send_rims(wide, side_send, side_recv, lat_send, lat_recv):
        last, first = pl.ds(WIDTH, 16), pl.ds(16, 16)
        left, right = pl.ds(0, 16), pl.ds(WIDTH + 16, 16)
        top, bottom = wide.at[1], wide.at[4]
        send(wide.at[inner, last], wide.at[inner, left], side_send, side_recv, (a, east))
        send(wide.at[inner, first], wide.at[inner, right], side_send, side_recv, (a, west))
        send(bottom.at[middle], wide.at[0, middle], lat_send, lat_recv, (south, b))
        send(top.at[middle], wide.at[5, middle], lat_send, lat_recv, (north, b))
        send(bottom.at[last], wide.at[0, left], lat_send, lat_recv, (south, east))
        send(bottom.at[first], wide.at[0, right], lat_send, lat_recv, (south, west))
        send(top.at[last], wide.at[5, left], lat_send, lat_recv, (north, east))
        send(top.at[first], wide.at[5, right], lat_send, lat_recv, (north, west))

    def side_size(wide):
        return wide.at[pl.ds(0, 4), pl.ds(0, 32), :]

    def lat_size(wide):
        return wide.at[pl.ds(0, 2), :, :]

    def to_lon(src, buf, kind):
        return [
            send(
                src,
                buf.at[d - 1],
                lon_sem.at[kind, 0, d - 1],
                lon_sem.at[kind, 1, d - 1],
                (a, lax.rem(b + d, LON)),
            )
            for d in range(1, LON)
        ]

    gain_copies = to_lon(gain_src, gain_buf, 0)
    loads[0].wait()
    send_rims(field_wide, sem.at[0], sem.at[1], sem.at[24], sem.at[25])
    loads[1].wait()
    loads[2].wait()
    pack_partial(1, 1, lambda i: cot_wide[i + 1, 16 : 16 + WIDTH, :], False)

    for copy in gain_copies:
        copy.wait()
    gain_row = gain_src[...].astype(F32)
    for d in range(LON - 1):
        gain_row = gain_row + gain_buf[d].astype(F32)
    gain_row = gain_row.astype(BF)
    for t in range(ORDERS):
        table_src[t, 0:16, :] = legendre_ref[t]
        table_src[t, 16:32, :] = gain_row

    def send_table(d, carry):
        to_z, to_x = lax.rem(z + d, 8), lax.rem(b + 1, 4)
        src = table_src.at[to_z * 2 + lax.div(to_x, 2)]
        dst = table_buf.at[z, y_lo, lax.div(x, 2), lax.rem(x, 2)]
        send(src, dst, sem.at[2], sem.at[3], (to_z * 8 + y_lo * 4 + to_x, x))
        return carry

    lax.fori_loop(0, 8, send_table, 0)
    send_partial(1, sem.at[26], sem.at[27], sem.at[28])

    for load in loads[3:6]:
        load.wait()
    entry = lax.broadcasted_iota(jnp.int32, (18, 128), 1)
    place_of = lax.broadcasted_iota(jnp.int32, (18, LATITUDES), 1)
    code = (support_tap_ref[...] * BASIS_COUNT + support_basis_ref[...]).astype(F32)
    columns = []
    for r in range(6):
        here = place_of == a * 4 + r - 1
        own_code = jnp.sum(jnp.where(here, code, 0.0), axis=1, keepdims=True)
        own_weight = jnp.sum(
            jnp.where(here, support_weight_ref[...], 0.0), axis=1, keepdims=True
        )
        kept = jnp.where(own_code == entry.astype(F32), own_weight, 0.0)
        columns.append(jnp.sum(kept, axis=0, keepdims=True).astype(BF).astype(F32))

    diagonal = lax.broadcasted_iota(jnp.int32, (96, 128), 1)
    diagonal = diagonal - lax.broadcasted_iota(jnp.int32, (96, 128), 0) - 15
    inside_north = jnp.where(a == 0, 0.0, 1.0)
    inside_south = jnp.where(a == LAT - 1, 0.0, 1.0)

    def make_band(dst, i, adjoint):
        for p in range(3):
            for k in range(BASIS_COUNT):
                block = jnp.zeros((96, 128), F32)
                for q in range(3):
                    if adjoint:
                        column, at = columns[i + p], (8 - 3 * p - q) * BASIS_COUNT + k
                    else:
                        column, at = columns[i + 1], (3 * p + q) * BASIS_COUNT + k
                    value = column[:, at : at + 1]
                    if not adjoint:
                        if i == 0 and p == 0:
                            value = value * inside_north
                        if i == 3 and p == 2:
                            value = value * inside_south
                    block = jnp.where(diagonal == q, value, block)
                dst[i, k * 96 : k * 96 + 96, p * 128 : p * 128 + 128] = block.astype(BF)

    for i in range(4):
        make_band(band, i, False)

    def stencil(src, bands, i, block):
        near = jnp.concatenate([src[i + p, block * 96 : block * 96 + 128, :] for p in range(3)])
        return jnp.dot(bands[i], near, preferred_element_type=F32).astype(BF)

    whole_wait(table_buf.at[:, 0, 0, 0], sem.at[3])
    column_block = table_buf.at[:, y_lo, y_hi, core]
    for d in range(1, 4):
        y = lax.rem(y_hi * 2 + y_lo + d, 4)
        peer = (z * 8 + lax.rem(y, 2) * 4 + x, lax.div(y, 2) * 2 + core)
        send(column_block, column_block, sem.at[31], sem.at[32], peer)

    def gather_modes(which, send_sem, recv_sem):
        total = part_buf[which, :, 0]
        for d in range(1, LON):
            total = total + part_buf[which, :, d]
        halves = [total, jnp.zeros_like(total)]
        if which == 1:
            halves.reverse()
        mode_buf[which, :, y_lo, b] = jnp.concatenate(halves, axis=1).astype(BF)
        own_modes = mode_buf.at[which, :, y_lo, b]
        for d in range(1, 8):
            g = lax.rem(y_lo * 4 + b + d, 8)
            peer = (z * 8 + lax.div(g, 4) * 4 + x, lax.rem(g, 4))
            send(own_modes, own_modes, send_sem, recv_sem, peer)

    wait_partial(1, sem.at[27], sem.at[28])
    gather_modes(1, sem.at[36], sem.at[8])

    loads[6].wait()
    whole_wait(side_size(field_wide), sem.at[1])

    def filter_cycle(i):
        for block in range(2):
            sums = stencil(field_wide, band, i, block)
            first = i * WIDTH + block * 96
            for k in range(BASIS_COUNT):
                filtered[first : first + 96, k * 256 : k * 256 + 256] = sums[k * 96 : k * 96 + 96]
        own = slice(i * WIDTH, i * WIDTH + WIDTH)
        mix = jnp.dot(filtered[own, :], filter_ref[...], preferred_element_type=F32)
        own_field = field_wide[i + 1, 16 : 16 + WIDTH, :].astype(F32)
        hidden[i] = (own_field + mix).astype(BF)

    filter_cycle(1)
    filter_cycle(2)

    whole_wait(lat_size(field_wide), sem.at[25])
    filter_cycle(0)
    filter_cycle(3)
    whole_wait(table_buf.at[pl.ds(0, 6), 0], sem.at[32])
    core_table = table_buf.at[:, :, :, core]
    table_copy = send(core_table, core_table, sem.at[34], sem.at[35], (a, other_core))
    pack_partial(0, 0, lambda i: hidden[i], True)
    send_partial(0, sem.at[7], sem.at[33], sem.at[9])


    send_rims(cot_wide, sem.at[5], sem.at[6], sem.at[29], sem.at[30])

    for load in loads[7:]:
        load.wait()
    table_copy.wait()
    for chunk in range(8):
        packed = table_buf[chunk].reshape(256, 128)
        for block in range(3):
            rows = jnp.dot(pick_ref[block], packed, preferred_element_type=F32)
            lanes = slice(block * 128, block * 128 + 128)
            rep[chunk, :, :, lanes] = rows.astype(BF).reshape(2, 64, 128)
            rep_t[lanes, chunk * 128 : chunk * 128 + 128] = rows.T.astype(BF)
        for side in range(2):
            rows = jnp.dot(gain_pick_ref[side], packed, preferred_element_type=F32)
            gain_all[chunk * 48 : chunk * 48 + 48, side * 128 : side * 128 + 128] = rows

    def tile(index):
        return pl.ds(pl.multiple_of(index * 16, 16), 16)

    def own_order(which, mode_recv, back_send, back_recv, own_sem):
        whole_wait(mode_buf.at[which, pl.ds(0, 7)], mode_recv)
        groups = (2 * which, 2 * which + 1)
        group = lax.rem(lax.div(lax.broadcasted_iota(jnp.int32, (1024, 128), 0), 4), 4)
        modes = mode_buf[which].reshape(1024, 128).astype(F32)
        for g in groups:
            kept = jnp.where(group == g, modes, 0.0).astype(BF)
            spec[:, g * 128 : g * 128 + 128] = jnp.dot(
                rep_t[...], kept, preferred_element_type=F32
            ).astype(BF)
        gains = gain_all[...]
        if which == 0:
            mix = jnp.dot(spec[:, 0:256], mixing_ref[...], preferred_element_type=F32)
            mixed[:, 0:256] = (gains * mix).astype(BF)
        else:
            scaled_s[...] = (gains * spec[:, 256:512].astype(F32)).astype(BF)
            mixed[:, 256:512] = lax.dot_general(
                scaled_s[...], mixing_ref[...], (((1,), (1,)), ((), ())), preferred_element_type=F32
            ).astype(BF)
        group = lax.rem(lax.div(lax.broadcasted_iota(jnp.int32, (512, 128), 0), 4), 4)
        rows = rep[:, y_lo].reshape(512, DEGREES)
        packed = jnp.zeros((512, 128), F32)
        for g in groups:
            sums = jnp.dot(rows, mixed[:, g * 128 : g * 128 + 128], preferred_element_type=F32)
            packed = jnp.where(group == g, sums, packed)
        back_src[which] = packed.astype(BF)

        def send_back(d, carry):
            to = lax.rem(slot + d, 32)
            src = back_src.at[which, tile(to), :]
            dst = cycle_buf.at[which, tile(slot), :]
            send(src, dst, back_send, back_recv, (row_peer(to), b))
            return carry

        lax.fori_loop(1, 32, send_back, 0)
        own_back = pltpu.make_async_copy(
            back_src.at[which, tile(slot), :], cycle_buf.at[which, tile(slot), :], own_sem
        )
        own_back.start()
        return own_back

    def wait_back(which, own_back, back_recv):
        own_back.wait()
        whole_wait(cycle_buf.at[which, pl.ds(0, 16 * 31), :], back_recv)
        cycle_wide[which] = cycle_buf[which].astype(F32)

    back_own = own_order(1, sem.at[8], sem.at[10], sem.at[11], sem.at[12])

    for k in range(BASIS_COUNT):
        for pair in range(2):
            rows = filtered[pair * 384 : pair * 384 + 384, k * 256 : k * 256 + 256]
            filtered_t[k * 256 : k * 256 + 256, pair * 384 : pair * 384 + 384] = rows.T
    for i in range(4):
        make_band(band_back, i, True)

    wait_partial(0, sem.at[33], sem.at[9])
    gather_modes(0, sem.at[37], sem.at[38])

    parts = ((1024, 256), (0, 512), (512, 512))

    def part_rows(n):
        return pl.ds(parts[n][0], parts[n][1])

    def piece(n, g):
        size = parts[n][1] // 16
        return pl.ds(pl.multiple_of(parts[n][0] + g * size, 16), size)

    def plane_slots(n, count):
        size = parts[n][1] // 16
        return pl.ds(parts[n][0] // 16 * 15, count * size)

    def core_send(n):
        rows = part_rows(n)
        core_src[rows, :] = terms[1 - core, rows, :].astype(BF)
        return send(
            core_src.at[rows],
            core_buf.at[rows],
            sum_sem.at[n, 0],
            sum_sem.at[n, 1],
            (a, other_core),
        )

    def plane_send(n, core_copy):
        rows, size = part_rows(n), parts[n][1] // 16
        core_copy.wait()
        plane_src[rows, :] = (terms[core, rows, :] + core_buf[rows, :].astype(F32)).astype(BF)

        def one(d, carry):
            g = lax.rem(place + d, 16)
            slot_rows = pl.ds(
                pl.multiple_of(parts[n][0] // 16 * 15 + (d - 1) * size, 16), size
            )
            send(
                plane_src.at[piece(n, g)],
                plane_buf.at[slot_rows],
                sum_sem.at[n, 2],
                sum_sem.at[n, 3],
                plane_peer(g),
            )
            return carry

        lax.fori_loop(1, 16, one, 0)

    def z_rows(n):
        return pl.ds(parts[n][0] // 16, parts[n][1] // 16)

    def z_send(n):
        size = parts[n][1] // 16
        whole_wait(plane_buf.at[plane_slots(n, 15)], sum_sem.at[n, 3])
        total = plane_src[piece(n, place), :].astype(F32)
        for d in range(15):
            first = parts[n][0] // 16 * 15 + d * size
            total = total + plane_buf[first : first + size, :].astype(F32)
        z_buf[z, z_rows(n), :] = total.astype(BF)
        mine = z_buf.at[z, z_rows(n)]

        def one(d, carry):
            send(mine, mine, sum_sem.at[n, 4], sum_sem.at[n, 5], z_peer(lax.rem(z + d, 8)))
            return carry

        lax.fori_loop(1, 8, one, 0)

    def z_size(n):
        return z_buf.at[pl.ds(0, 7), z_rows(n)]

    def gather_send(n):
        whole_wait(z_size(n), sum_sem.at[n, 5])
        total = z_buf[0, z_rows(n), :].astype(F32)
        for g in range(1, 8):
            total = total + z_buf[g, z_rows(n), :].astype(F32)
        sums_ref[core, piece(n, place), :] = total.astype(BF)
        mine = sums_ref.at[core, piece(n, place)]

        def one(d, carry):
            send(
                mine,
                mine,
                sum_sem.at[n, 6],
                sum_sem.at[n, 7],
                plane_peer(lax.rem(place + d, 16)),
            )
            return carry

        lax.fori_loop(1, 16, one, 0)

    def last_send(n):
        whole_wait(plane_buf.at[plane_slots(n, 15)], sum_sem.at[n, 7])
        half_sums = sums_ref.at[core, part_rows(n)]
        return send(half_sums, half_sums, sum_sem.at[n, 8], sum_sem.at[n, 9], (a, other_core))

    wait_back(1, back_own, sem.at[11])

    def cycle_rows(which, i):
        return jnp.concatenate(
            [cycle_wide[which, pl.ds(which * 8 + h * 4 + i, 32, stride=16), :] for h in range(2)], axis=1
        )

    for i in (0, 3, 1, 2):
        near_cycles[i + 1] = (cycle_rows(1, i) * cycle_weight_ref[i]).astype(BF)
    near_copies = [
        send(near_cycles.at[1], near_cycles.at[5], near_sem.at[0], near_sem.at[1], (north, b)),
        send(near_cycles.at[4], near_cycles.at[0], near_sem.at[2], near_sem.at[3], (south, b)),
    ]

    def make_grad(r):
        spatial = jnp.dot(wide_ref[0], near_cycles[r], preferred_element_type=F32).astype(BF)
        return (cot_wide[r].astype(F32) + spatial.astype(F32)).astype(BF)

    whole_wait(side_size(cot_wide), sem.at[6])
    whole_wait(lat_size(cot_wide), sem.at[30])
    for i in range(4):
        grad = make_grad(i + 1)
        grad_wide[i + 1] = grad
        grad_own[i * WIDTH : i * WIDTH + WIDTH, :] = grad[16 : 16 + WIDTH]
    def filter_terms(k):
        own = slice(k * 256, k * 256 + 256)
        term = jnp.dot(filtered_t[own, :], grad_own[...], preferred_element_type=F32)
        for h in range(2):
            terms[h, own, :] = term[:, h * 128 : h * 128 + 128]

    filter_terms(0)
    filter_terms(1)
    first_copy = core_send(1)
    filter_terms(2)
    filter_terms(3)
    second_copy = core_send(2)
    fore_own = own_order(0, sem.at[38], sem.at[39], sem.at[40], sem.at[41])
    plane_send(1, first_copy)

    degrees = pl.ds(pl.multiple_of((y_lo * 4 + b) * 48, 16), 48)
    term = lax.dot_general(
        spec[degrees, 0:256],
        scaled_s[degrees, :],
        (((0,), (0,)), ((), ())),
        preferred_element_type=F32,
    )
    for h in range(2):
        terms[h, 1024:1280, :] = term[:, h * 128 : h * 128 + 128]

    spectral_copy = core_send(0)
    plane_send(2, second_copy)

    def finish_output(i):
        fore = cycle_rows(0, i).astype(BF)
        spatial = jnp.dot(wide_ref[1, 16 : 16 + WIDTH, :], fore, preferred_element_type=F32)
        out_ref[i] = (hidden[i].astype(F32) + spatial.astype(BF).astype(F32)).astype(BF)

    for copy in near_copies:
        copy.wait()
    for r in (0, 5):
        grad_wide[r] = make_grad(r)

    def field_grad(i):
        total = grad_own[i * WIDTH : i * WIDTH + WIDTH, :].astype(F32)
        done = []
        for block in range(2):
            sums = stencil(grad_wide, band_back, i, block)
            part = total[block * 96 : block * 96 + 96]
            for k in range(BASIS_COUNT):
                part = part + lax.dot_general(
                    sums[k * 96 : k * 96 + 96],
                    filter_ref[k * 256 : k * 256 + 256, :],
                    (((1,), (1,)), ((), ())),
                    preferred_element_type=F32,
                )
            done.append(part)
        grad_ref[i] = jnp.concatenate(done).astype(BF)

    z_send(1)
    field_grad(0)
    plane_send(0, spectral_copy)
    z_send(2)
    field_grad(1)
    gather_send(1)
    z_send(0)
    field_grad(2)
    gather_send(2)
    field_grad(3)
    gather_send(0)
    last_copies = [last_send(1)]
    wait_back(0, fore_own, sem.at[40])
    for i in range(4):
        finish_output(i)
    last_copies.append(last_send(2))
    last_copies.append(last_send(0))

    whole_wait(side_size(field_wide), sem.at[0])
    whole_wait(lat_size(field_wide), sem.at[24])
    whole_wait(side_size(cot_wide), sem.at[5])
    whole_wait(lat_size(cot_wide), sem.at[29])
    wait_partial(1, sem.at[26], None)
    wait_partial(0, sem.at[7], None)
    whole_wait(table_buf.at[:, 0, 0, 0], sem.at[2])
    whole_wait(table_buf.at[pl.ds(0, 6), 0], sem.at[31])
    whole_wait(mode_buf.at[0, pl.ds(0, 7)], sem.at[36])
    whole_wait(mode_buf.at[0, pl.ds(0, 7)], sem.at[37])
    whole_wait(cycle_buf.at[0, pl.ds(0, 16 * 31), :], sem.at[10])
    whole_wait(cycle_buf.at[0, pl.ds(0, 16 * 31), :], sem.at[39])
    for n in range(3):
        whole_wait(plane_buf.at[plane_slots(n, 15)], sum_sem.at[n, 2])
        whole_wait(z_size(n), sum_sem.at[n, 4])
        whole_wait(plane_buf.at[plane_slots(n, 15)], sum_sem.at[n, 6])
    for copy in last_copies:
        copy.wait()


def finish_kernel(sums_hbm, out_hbm, grad_hbm, out_ref, grad_ref, filter_ref, spectral_ref, *scratch):
    sums_ref, filter_vmem, spectral_vmem, out_vmem, grad_vmem, sem = scratch
    b = lax.axis_index("lon")
    copies = [
        pltpu.make_async_copy(sums_hbm, sums_ref, sem.at[0]),
        pltpu.make_async_copy(out_hbm, out_vmem, sem.at[1]),
        pltpu.make_async_copy(grad_hbm, grad_vmem, sem.at[2]),
    ]
    for copy in copies:
        copy.start()
    copies[0].wait()
    grid_scale = (LATITUDES * LONGITUDES) ** (-0.5)
    for k in range(BASIS_COUNT):
        for h in range(2):
            rows, lanes = slice(k * 256, k * 256 + 256), slice(h * 128, h * 128 + 128)
            filter_vmem[rows, lanes] = sums_ref[h, rows, :].astype(F32) * grid_scale
        rows = pl.ds(k * 256, 256)
        copies.append(
            pltpu.make_async_copy(filter_vmem.at[rows], filter_ref.at[rows], sem.at[3 + k])
        )
        copies[-1].start()
    columns = sums_ref[lax.div(b, 2), 1024:1280, :].astype(F32)
    columns = columns * (2 * ORDERS * DEGREES) ** (-0.5)
    spectral_vmem[...] = jnp.where(
        lax.rem(b, 2) == 0, columns[:, 0:64], columns[:, 64:128]
    ).T
    copies.append(pltpu.make_async_copy(spectral_vmem, spectral_ref, sem.at[7]))
    copies[-1].start()
    for n, (staged, target) in enumerate(((out_vmem, out_ref), (grad_vmem, grad_ref))):
        copies[1 + n].wait()
        copies.append(pltpu.make_async_copy(staged, target, sem.at[8 + n]))
        copies[-1].start()
    for copy in copies[3:]:
        copy.wait()


def finish_call(sums, out, grad):
    anywhere = pl.BlockSpec(memory_space=pl.ANY)
    return pl.pallas_call(
        finish_kernel,
        out_shape=(
            jax.ShapeDtypeStruct((4, WIDTH, 256), BF),
            jax.ShapeDtypeStruct((4, WIDTH, 256), BF),
            jax.ShapeDtypeStruct((1024, 256), F32),
            jax.ShapeDtypeStruct((64, 256), F32),
        ),
        in_specs=[anywhere] * 3,
        out_specs=(anywhere,) * 4,
        scratch_shapes=[
            pltpu.VMEM((2, ROWS, 128), BF),
            pltpu.VMEM((1024, 256), F32),
            pltpu.VMEM((64, 256), F32),
            pltpu.VMEM((4, WIDTH, 256), BF),
            pltpu.VMEM((4, WIDTH, 256), BF),
            pltpu.SemaphoreType.DMA((10,)),
        ],
        compiler_params=pltpu.CompilerParams(vmem_limit_bytes=60 * 2**20),
        name="finish",
    )(sums, out, grad)


def block_call(cycle_weight, field, cotangent, legendre, gain, mixing, filter_weight, support):
    pick, gain_pick = unpack_constants()
    wide, across = trig_tables()
    vmem = pl.BlockSpec(memory_space=pltpu.VMEM)
    smem = pl.BlockSpec(memory_space=pltpu.SMEM)
    anywhere = pl.BlockSpec(memory_space=pl.ANY)
    dma = pltpu.SemaphoreType.DMA
    return pl.pallas_call(
        block_kernel,
        out_shape=(
            jax.ShapeDtypeStruct((4, WIDTH, 256), BF),
            jax.ShapeDtypeStruct((4, WIDTH, 256), BF),
            jax.ShapeDtypeStruct((2, ROWS, 128), BF),
        ),
        in_specs=[smem, anywhere, anywhere, vmem, vmem] + [anywhere] * 9,
        out_specs=(vmem,) * 3,
        scratch_shapes=[
            pltpu.VMEM((256, 256), BF),
            pltpu.VMEM((1024, 256), BF),
            pltpu.VMEM((3, 128, 256), BF),
            pltpu.VMEM((2, 48, 256), BF),
            pltpu.VMEM((2, WIDE, 32), BF),
            pltpu.VMEM((2, 32, WIDTH), BF),
            pltpu.VMEM((18, LATITUDES), jnp.int32),
            pltpu.VMEM((18, LATITUDES), jnp.int32),
            pltpu.VMEM((18, LATITUDES), F32),
            pltpu.VMEM((6, WIDE, 256), BF),
            pltpu.VMEM((6, WIDE, 256), BF),
            pltpu.VMEM((6, WIDE, 256), BF),
            pltpu.VMEM((4, 384, 384), BF),
            pltpu.VMEM((4, 384, 384), BF),
            pltpu.VMEM((768, 1024), BF),
            pltpu.VMEM((1024, 768), BF),
            pltpu.VMEM((4, WIDTH, 256), BF),
            pltpu.VMEM((768, 256), BF),
            pltpu.VMEM((2, 256, 128), F32),
            pltpu.VMEM((2, 8, LON, 8, 128), F32),
            pltpu.VMEM((16, 128), F32),
            pltpu.VMEM((16, 128), BF),
            pltpu.VMEM((3, 16, 128), BF),
            pltpu.VMEM((16, 32, 128), BF),
            pltpu.VMEM((8, 2, 2, 2, 32, 128), BF),
            pltpu.VMEM((2, 8, 2, 4, 16, 128), BF),
            pltpu.VMEM((8, 2, 64, DEGREES), BF),
            pltpu.VMEM((DEGREES, 1024), BF),
            pltpu.VMEM((DEGREES, 256), F32),
            pltpu.VMEM((DEGREES, 512), BF),
            pltpu.VMEM((DEGREES, 256), BF),
            pltpu.VMEM((DEGREES, 512), BF),
            pltpu.VMEM((2, 512, 128), BF),
            pltpu.VMEM((2, 512, 128), BF),
            pltpu.VMEM((2, 512, 128), F32),
            pltpu.VMEM((6, 32, 256), BF),
            pltpu.VMEM((2, ROWS, 128), F32),
            pltpu.VMEM((ROWS, 128), BF),
            pltpu.VMEM((ROWS, 128), BF),
            pltpu.VMEM((ROWS, 128), BF),
            pltpu.VMEM((15 * PIECE, 128), BF),
            pltpu.VMEM((8, PIECE, 128), BF),
            dma((42,)),
            dma((1, 2, 3)),
            dma((4,)),
            dma((11,)),
            dma((3, 10)),
        ],
        compiler_params=pltpu.CompilerParams(
            collective_id=0, has_side_effects=True, vmem_limit_bytes=60 * 2**20
        ),
        name="block",
    )(
        cycle_weight,
        field,
        cotangent,
        legendre,
        gain,
        mixing,
        filter_weight,
        jnp.asarray(pick, BF),
        jnp.asarray(gain_pick, BF),
        jnp.asarray(wide, BF),
        jnp.asarray(across, BF),
        *support,
    )


def per_device(
    field,
    cotangent,
    legendre,
    cycle_weight,
    support_tap,
    support_basis,
    support_weight,
    filter_weight,
    spectral_weight,
    spectral_gain,
):
    table = legendre.reshape(16, 3, 128, 4).transpose(0, 1, 3, 2).reshape(16, 12, 128)
    table = jnp.pad(table, ((0, 0), (0, 4), (0, 0)))
    output, grad_field, sums = block_call(
        cycle_weight,
        field,
        cotangent,
        table,
        spectral_gain,
        spectral_weight,
        filter_weight.reshape(1024, 256),
        (support_tap.T, support_basis.T, support_weight.T),
    )
    output, grad_field, grad_filter, grad_spectral = finish_call(sums, output, grad_field)
    return (output, grad_field, grad_filter.reshape(4, 256, 256), grad_spectral.T)


def solution(mesh):
    placed = (
        P("lat", "lon", None),
        P("lat", "lon", None),
        P(None, None, "lat"),
        P("lat"),
        P(),
        P(),
        P(),
        P(),
        P(),
        P("lat", "lon"),
    )
    return jax.shard_map(
        per_device,
        mesh=mesh,
        in_specs=placed,
        out_specs=(P("lat", "lon", None), P("lat", "lon", None), P(), P(None, "lon")),
        check_vma=False,
    )
```

```python
import math

import jax
import jax.numpy as jnp
import numpy as np
from jax import lax
from jax.experimental import pallas as pl
from jax.experimental.pallas import tpu as pltpu
from jax.sharding import PartitionSpec as P

LATITUDES = 256
LONGITUDES = 768
DEGREES = 384
ORDERS = 16
BASIS_COUNT = 4
LAT = 64
LON = 4
WIDTH = LONGITUDES // LON
WIDE = WIDTH + 32
ROWS = 1280
PIECE = 80
MESH = pl.DeviceIdType.MESH
BF = jnp.bfloat16
F32 = jnp.float32


def trig_tables():
    longitude = np.arange(LONGITUDES)
    order = np.arange(ORDERS)
    angle = (longitude[:, None] * order[None, :] % LONGITUDES) * (2.0 * math.pi / LONGITUDES)
    table = np.stack([np.cos(angle), np.sin(angle)], axis=2).reshape(LONGITUDES, 2 * ORDERS)
    both = np.stack([table * LONGITUDES ** (-0.5), table * (2 * ORDERS) ** (-0.5)])
    both = both.astype(np.float32)
    where = np.arange(LON)[:, None] * WIDTH + np.arange(-16, WIDTH + 16)[None, :]
    wide = both[:, where % LONGITUDES].transpose(1, 0, 2, 3)
    across = wide[:, :, 16 : 16 + WIDTH].transpose(0, 1, 3, 2)
    return wide, across


def whole_wait(ref, sem):
    pltpu.make_async_copy(ref, ref, sem).wait()


def unpack_constants():
    pick = np.zeros((3, 128, 256), np.float32)
    gain_pick = np.zeros((2, 48, 256), np.float32)
    for dev in range(8):
        for block in range(3):
            for group in range(4):
                for cycle in range(4):
                    pick[block, dev * 16 + group * 4 + cycle, dev * 32 + block * 4 + cycle] = 1.0
        for half in range(2):
            for degree in range(6):
                gain_pick[half, dev * 6 + degree, dev * 32 + 16 + half * 6 + degree] = 1.0
    return pick, gain_pick


def block_kernel(
    cycle_weight_ref,
    field_ref,
    cot_ref,
    legendre_ref,
    gain_ref,
    mixing_hbm,
    filter_hbm,
    pick_hbm,
    gain_pick_hbm,
    wide_hbm,
    across_hbm,
    support_tap_hbm,
    support_basis_hbm,
    support_weight_hbm,
    out_ref,
    grad_ref,
    sums_ref,
    mixing_ref,
    filter_ref,
    pick_ref,
    gain_pick_ref,
    wide_ref,
    across_ref,
    support_tap_ref,
    support_basis_ref,
    support_weight_ref,
    field_wide,
    cot_wide,
    grad_wide,
    band,
    band_back,
    filtered,
    filtered_t,
    hidden,
    grad_own,
    partial,
    part_buf,
    gain_wide,
    gain_src,
    gain_buf,
    table_src,
    table_buf,
    mode_buf,
    rep,
    rep_t,
    gain_all,
    spec,
    scaled_s,
    mixed,
    back_src,
    cycle_buf,
    cycle_wide,
    near_cycles,
    terms,
    core_src,
    core_buf,
    plane_src,
    plane_buf,
    z_buf,
    sem,
    lon_sem,
    near_sem,
    load_sem,
    sum_sem,
):
    a = lax.axis_index("lat")
    b = lax.axis_index("lon")
    x = lax.rem(a, 4)
    y_lo = lax.rem(lax.div(a, 4), 2)
    z = lax.div(a, 8)
    core = lax.rem(b, 2)
    y_hi = lax.div(b, 2)
    place = (y_hi * 2 + y_lo) * 4 + x
    other_core = y_hi * 2 + 1 - core
    north, south = lax.rem(a + LAT - 1, LAT), lax.rem(a + 1, LAT)
    west, east = lax.rem(b + LON - 1, LON), lax.rem(b + 1, LON)
    slot = z * 4 + x
    barrier = pltpu.get_barrier_semaphore()

    def plane_peer(g):
        py, px = lax.div(g, 4), lax.rem(g, 4)
        return (z * 8 + lax.rem(py, 2) * 4 + px, lax.div(py, 2) * 2 + core)

    def z_peer(g):
        return (g * 8 + y_lo * 4 + x, b)

    def greet(device):
        pl.semaphore_signal(barrier, inc=1, device_id=device, device_id_type=MESH)

    def row_peer(index):
        return lax.div(index, 4) * 8 + y_lo * 4 + lax.rem(index, 4)

    def greet_row(d, carry):
        greet((row_peer(lax.rem(slot + d, 32)), b))
        return carry

    def greet_source(d, carry):
        greet((lax.div(d, 4) * 8 + y_lo * 4 + b, lax.rem(d, 4)))
        return carry

    def greet_plane(d, carry):
        greet(plane_peer(lax.rem(place + d, 16)))
        return carry

    for d in range(1, LON):
        greet((a, lax.rem(b + d, LON)))
    for d in range(LON):
        greet((z * 8 + (1 - y_lo) * 4 + x, d))
    for lat in (north, south):
        greet((lat, b))
        for lon in (west, east):
            greet((lat, lon))
    lax.fori_loop(1, 16, greet_plane, 0)
    lax.fori_loop(1, 32, greet_row, 0)

    @pl.when(b == x)
    def greet_sources_but_me():
        def one(d, carry):
            index = lax.rem(z * 4 + b + d, 32)
            return greet_source(index, carry)

        lax.fori_loop(1, 32, one, 0)

    @pl.when(b != x)
    def greet_sources():
        lax.fori_loop(0, 32, greet_source, 0)

    def send(src, dst, send_sem, recv_sem, device):
        copy = pltpu.make_async_remote_copy(
            src_ref=src,
            dst_ref=dst,
            send_sem=send_sem,
            recv_sem=recv_sem,
            device_id=device,
            device_id_type=MESH,
        )
        copy.start()
        return copy

    inner, middle = pl.ds(1, 4), pl.ds(16, WIDTH)
    loads = [
        pltpu.make_async_copy(src, dst, load_sem.at[n])
        for n, (src, dst) in enumerate(
            (
                (field_ref, field_wide.at[inner, middle, :]),
                (cot_ref, cot_wide.at[inner, middle, :]),
                (across_hbm.at[b], across_ref),
                (support_tap_hbm, support_tap_ref),
                (support_basis_hbm, support_basis_ref),
                (support_weight_hbm, support_weight_ref),
                (filter_hbm, filter_ref),
                (pick_hbm, pick_ref),
                (gain_pick_hbm, gain_pick_ref),
                (mixing_hbm, mixing_ref),
                (wide_hbm.at[b], wide_ref),
            )
        )
    ]
    for load in loads:
        load.start()

    lane = lax.broadcasted_iota(jnp.int32, (6, 128), 1)
    own_gain = gain_ref[...].astype(F32)
    own_gain = jnp.concatenate([own_gain, own_gain], axis=1)
    own_gain = jnp.where(lax.div(lane, 64) == core, own_gain, 0.0)
    gain_wide[...] = jnp.zeros((16, 128), F32)
    for h in range(2):
        gain_wide[h * 6 : h * 6 + 6, :] = jnp.where(y_hi == h, own_gain, 0.0)
    gain_src[...] = gain_wide[...].astype(BF)

    def pack_partial(which, table, rows, scale):
        for i in range(4):
            sums = jnp.dot(across_ref[table], rows(i), preferred_element_type=F32)
            if scale:
                sums = sums * cycle_weight_ref[i]
            for h in range(2):
                partial[which, pl.ds(h * 4 + i, 32, stride=8), :] = sums[:, h * 128 : h * 128 + 128]

    def eight(index):
        return pl.ds(pl.multiple_of(index * 8, 8), 8)

    def send_partial(which, send_sem, recv_sem, own_sem):
        def remote(tr):
            src, dst = partial.at[which, eight(tr), :], part_buf.at[which, z, b]
            send(src, dst, send_sem, recv_sem, (row_peer(tr), x))

        def one(d, carry):
            remote(lax.rem(slot + d, 32))
            return carry

        @pl.when(b == x)
        def to_me():
            pltpu.make_async_copy(
                partial.at[which, eight(slot), :], part_buf.at[which, z, b], own_sem
            ).start()

        @pl.when(b != x)
        def to_peer():
            remote(slot)

        lax.fori_loop(1, 32, one, 0)

    def partial_size(which, count):
        return partial.at[which, pl.ds(0, 8 * count), :]

    def wait_partial(which, send_or_recv_sem, own_sem):
        @pl.when(b == x)
        def with_mine():
            if own_sem is not None:
                whole_wait(partial_size(which, 1), own_sem)
            whole_wait(partial_size(which, 31), send_or_recv_sem)

        @pl.when(b != x)
        def without():
            whole_wait(partial_size(which, 32), send_or_recv_sem)

    pl.semaphore_wait(barrier, 3 + 4 + 6 + 15 + 31 + 32 - jnp.where(b == x, 1, 0))

    def send_rims(wide, side_send, side_recv, lat_send, lat_recv):
        last, first = pl.ds(WIDTH, 16), pl.ds(16, 16)
        left, right = pl.ds(0, 16), pl.ds(WIDTH + 16, 16)
        top, bottom = wide.at[1], wide.at[4]
        send(wide.at[inner, last], wide.at[inner, left], side_send, side_recv, (a, east))
        send(wide.at[inner, first], wide.at[inner, right], side_send, side_recv, (a, west))
        send(bottom.at[middle], wide.at[0, middle], lat_send, lat_recv, (south, b))
        send(top.at[middle], wide.at[5, middle], lat_send, lat_recv, (north, b))
        send(bottom.at[last], wide.at[0, left], lat_send, lat_recv, (south, east))
        send(bottom.at[first], wide.at[0, right], lat_send, lat_recv, (south, west))
        send(top.at[last], wide.at[5, left], lat_send, lat_recv, (north, east))
        send(top.at[first], wide.at[5, right], lat_send, lat_recv, (north, west))

    def side_size(wide):
        return wide.at[pl.ds(0, 4), pl.ds(0, 32), :]

    def lat_size(wide):
        return wide.at[pl.ds(0, 2), :, :]

    def to_lon(src, buf, kind):
        return [
            send(
                src,
                buf.at[d - 1],
                lon_sem.at[kind, 0, d - 1],
                lon_sem.at[kind, 1, d - 1],
                (a, lax.rem(b + d, LON)),
            )
            for d in range(1, LON)
        ]

    gain_copies = to_lon(gain_src, gain_buf, 0)
    loads[0].wait()
    send_rims(field_wide, sem.at[0], sem.at[1], sem.at[24], sem.at[25])
    loads[1].wait()
    loads[2].wait()
    pack_partial(1, 1, lambda i: cot_wide[i + 1, 16 : 16 + WIDTH, :], False)

    for copy in gain_copies:
        copy.wait()
    gain_row = gain_src[...].astype(F32)
    for d in range(LON - 1):
        gain_row = gain_row + gain_buf[d].astype(F32)
    gain_row = gain_row.astype(BF)
    for t in range(ORDERS):
        table_src[t, 0:16, :] = legendre_ref[t]
        table_src[t, 16:32, :] = gain_row

    def send_table(d, carry):
        to_z, to_x = lax.rem(z + d, 8), lax.rem(b + 1, 4)
        src = table_src.at[to_z * 2 + lax.div(to_x, 2)]
        dst = table_buf.at[z, y_lo, lax.div(x, 2), lax.rem(x, 2)]
        send(src, dst, sem.at[2], sem.at[3], (to_z * 8 + y_lo * 4 + to_x, x))
        return carry

    lax.fori_loop(0, 8, send_table, 0)
    send_partial(1, sem.at[26], sem.at[27], sem.at[28])

    for load in loads[3:6]:
        load.wait()
    entry = lax.broadcasted_iota(jnp.int32, (18, 128), 1)
    place_of = lax.broadcasted_iota(jnp.int32, (18, LATITUDES), 1)
    code = (support_tap_ref[...] * BASIS_COUNT + support_basis_ref[...]).astype(F32)
    columns = []
    for r in range(6):
        here = place_of == a * 4 + r - 1
        own_code = jnp.sum(jnp.where(here, code, 0.0), axis=1, keepdims=True)
        own_weight = jnp.sum(
            jnp.where(here, support_weight_ref[...], 0.0), axis=1, keepdims=True
        )
        kept = jnp.where(own_code == entry.astype(F32), own_weight, 0.0)
        columns.append(jnp.sum(kept, axis=0, keepdims=True).astype(BF).astype(F32))

    diagonal = lax.broadcasted_iota(jnp.int32, (96, 128), 1)
    diagonal = diagonal - lax.broadcasted_iota(jnp.int32, (96, 128), 0) - 15
    inside_north = jnp.where(a == 0, 0.0, 1.0)
    inside_south = jnp.where(a == LAT - 1, 0.0, 1.0)

    def make_band(dst, i, adjoint):
        for p in range(3):
            for k in range(BASIS_COUNT):
                block = jnp.zeros((96, 128), F32)
                for q in range(3):
                    if adjoint:
                        column, at = columns[i + p], (8 - 3 * p - q) * BASIS_COUNT + k
                    else:
                        column, at = columns[i + 1], (3 * p + q) * BASIS_COUNT + k
                    value = column[:, at : at + 1]
                    if not adjoint:
                        if i == 0 and p == 0:
                            value = value * inside_north
                        if i == 3 and p == 2:
                            value = value * inside_south
                    block = jnp.where(diagonal == q, value, block)
                dst[i, k * 96 : k * 96 + 96, p * 128 : p * 128 + 128] = block.astype(BF)

    for i in range(4):
        make_band(band, i, False)

    def stencil(src, bands, i, block):
        near = jnp.concatenate([src[i + p, block * 96 : block * 96 + 128, :] for p in range(3)])
        return jnp.dot(bands[i], near, preferred_element_type=F32).astype(BF)

    whole_wait(table_buf.at[:, 0, 0, 0], sem.at[3])
    column_block = table_buf.at[:, y_lo, y_hi, core]
    for d in range(1, 4):
        y = lax.rem(y_hi * 2 + y_lo + d, 4)
        peer = (z * 8 + lax.rem(y, 2) * 4 + x, lax.div(y, 2) * 2 + core)
        send(column_block, column_block, sem.at[31], sem.at[32], peer)

    def gather_modes(which, send_sem, recv_sem):
        total = part_buf[which, :, 0]
        for d in range(1, LON):
            total = total + part_buf[which, :, d]
        halves = [total, jnp.zeros_like(total)]
        if which == 1:
            halves.reverse()
        mode_buf[which, :, y_lo, b] = jnp.concatenate(halves, axis=1).astype(BF)
        own_modes = mode_buf.at[which, :, y_lo, b]
        for d in range(1, 8):
            g = lax.rem(y_lo * 4 + b + d, 8)
            peer = (z * 8 + lax.div(g, 4) * 4 + x, lax.rem(g, 4))
            send(own_modes, own_modes, send_sem, recv_sem, peer)

    wait_partial(1, sem.at[27], sem.at[28])
    gather_modes(1, sem.at[36], sem.at[8])

    loads[6].wait()
    whole_wait(side_size(field_wide), sem.at[1])

    def filter_cycle(i):
        for block in range(2):
            sums = stencil(field_wide, band, i, block)
            first = i * WIDTH + block * 96
            for k in range(BASIS_COUNT):
                filtered[first : first + 96, k * 256 : k * 256 + 256] = sums[k * 96 : k * 96 + 96]
        own = slice(i * WIDTH, i * WIDTH + WIDTH)
        mix = jnp.dot(filtered[own, :], filter_ref[...], preferred_element_type=F32)
        own_field = field_wide[i + 1, 16 : 16 + WIDTH, :].astype(F32)
        hidden[i] = (own_field + mix).astype(BF)

    filter_cycle(1)
    filter_cycle(2)

    whole_wait(lat_size(field_wide), sem.at[25])
    filter_cycle(0)
    filter_cycle(3)
    whole_wait(table_buf.at[pl.ds(0, 6), 0], sem.at[32])
    core_table = table_buf.at[:, :, :, core]
    table_copy = send(core_table, core_table, sem.at[34], sem.at[35], (a, other_core))
    pack_partial(0, 0, lambda i: hidden[i], True)
    send_partial(0, sem.at[7], sem.at[33], sem.at[9])


    send_rims(cot_wide, sem.at[5], sem.at[6], sem.at[29], sem.at[30])

    for load in loads[7:]:
        load.wait()
    table_copy.wait()
    for chunk in range(8):
        packed = table_buf[chunk].reshape(256, 128)
        for block in range(3):
            rows = jnp.dot(pick_ref[block], packed, preferred_element_type=F32)
            lanes = slice(block * 128, block * 128 + 128)
            rep[chunk, :, :, lanes] = rows.astype(BF).reshape(2, 64, 128)
            rep_t[lanes, chunk * 128 : chunk * 128 + 128] = rows.T.astype(BF)
        for side in range(2):
            rows = jnp.dot(gain_pick_ref[side], packed, preferred_element_type=F32)
            gain_all[chunk * 48 : chunk * 48 + 48, side * 128 : side * 128 + 128] = rows

    def tile(index):
        return pl.ds(pl.multiple_of(index * 16, 16), 16)

    def own_order(which, mode_recv, back_send, back_recv, own_sem):
        whole_wait(mode_buf.at[which, pl.ds(0, 7)], mode_recv)
        groups = (2 * which, 2 * which + 1)
        group = lax.rem(lax.div(lax.broadcasted_iota(jnp.int32, (1024, 128), 0), 4), 4)
        modes = mode_buf[which].reshape(1024, 128).astype(F32)
        for g in groups:
            kept = jnp.where(group == g, modes, 0.0).astype(BF)
            spec[:, g * 128 : g * 128 + 128] = jnp.dot(
                rep_t[...], kept, preferred_element_type=F32
            ).astype(BF)
        gains = gain_all[...]
        if which == 0:
            mix = jnp.dot(spec[:, 0:256], mixing_ref[...], preferred_element_type=F32)
            mixed[:, 0:256] = (gains * mix).astype(BF)
        else:
            scaled_s[...] = (gains * spec[:, 256:512].astype(F32)).astype(BF)
            mixed[:, 256:512] = lax.dot_general(
                scaled_s[...], mixing_ref[...], (((1,), (1,)), ((), ())), preferred_element_type=F32
            ).astype(BF)
        group = lax.rem(lax.div(lax.broadcasted_iota(jnp.int32, (512, 128), 0), 4), 4)
        rows = rep[:, y_lo].reshape(512, DEGREES)
        packed = jnp.zeros((512, 128), F32)
        for g in groups:
            sums = jnp.dot(rows, mixed[:, g * 128 : g * 128 + 128], preferred_element_type=F32)
            packed = jnp.where(group == g, sums, packed)
        back_src[which] = packed.astype(BF)

        def send_back(d, carry):
            to = lax.rem(slot + d, 32)
            src = back_src.at[which, tile(to), :]
            dst = cycle_buf.at[which, tile(slot), :]
            send(src, dst, back_send, back_recv, (row_peer(to), b))
            return carry

        lax.fori_loop(1, 32, send_back, 0)
        own_back = pltpu.make_async_copy(
            back_src.at[which, tile(slot), :], cycle_buf.at[which, tile(slot), :], own_sem
        )
        own_back.start()
        return own_back

    def wait_back(which, own_back, back_recv):
        own_back.wait()
        whole_wait(cycle_buf.at[which, pl.ds(0, 16 * 31), :], back_recv)
        cycle_wide[which] = cycle_buf[which].astype(F32)

    back_own = own_order(1, sem.at[8], sem.at[10], sem.at[11], sem.at[12])

    for k in range(BASIS_COUNT):
        for pair in range(2):
            rows = filtered[pair * 384 : pair * 384 + 384, k * 256 : k * 256 + 256]
            filtered_t[k * 256 : k * 256 + 256, pair * 384 : pair * 384 + 384] = rows.T
    for i in range(4):
        make_band(band_back, i, True)

    wait_partial(0, sem.at[33], sem.at[9])
    gather_modes(0, sem.at[37], sem.at[38])

    parts = ((1024, 256), (0, 512), (512, 512))

    def part_rows(n):
        return pl.ds(parts[n][0], parts[n][1])

    def piece(n, g):
        size = parts[n][1] // 16
        return pl.ds(pl.multiple_of(parts[n][0] + g * size, 16), size)

    def plane_slots(n, count):
        size = parts[n][1] // 16
        return pl.ds(parts[n][0] // 16 * 15, count * size)

    def core_send(n):
        rows = part_rows(n)
        core_src[rows, :] = terms[1 - core, rows, :].astype(BF)
        return send(
            core_src.at[rows],
            core_buf.at[rows],
            sum_sem.at[n, 0],
            sum_sem.at[n, 1],
            (a, other_core),
        )

    def plane_send(n, core_copy):
        rows, size = part_rows(n), parts[n][1] // 16
        core_copy.wait()
        plane_src[rows, :] = (terms[core, rows, :] + core_buf[rows, :].astype(F32)).astype(BF)

        def one(d, carry):
            g = lax.rem(place + d, 16)
            slot_rows = pl.ds(
                pl.multiple_of(parts[n][0] // 16 * 15 + (d - 1) * size, 16), size
            )
            send(
                plane_src.at[piece(n, g)],
                plane_buf.at[slot_rows],
                sum_sem.at[n, 2],
                sum_sem.at[n, 3],
                plane_peer(g),
            )
            return carry

        lax.fori_loop(1, 16, one, 0)

    def z_rows(n):
        return pl.ds(parts[n][0] // 16, parts[n][1] // 16)

    def z_send(n):
        size = parts[n][1] // 16
        whole_wait(plane_buf.at[plane_slots(n, 15)], sum_sem.at[n, 3])
        total = plane_src[piece(n, place), :].astype(F32)
        for d in range(15):
            first = parts[n][0] // 16 * 15 + d * size
            total = total + plane_buf[first : first + size, :].astype(F32)
        z_buf[z, z_rows(n), :] = total.astype(BF)
        mine = z_buf.at[z, z_rows(n)]

        def one(d, carry):
            send(mine, mine, sum_sem.at[n, 4], sum_sem.at[n, 5], z_peer(lax.rem(z + d, 8)))
            return carry

        lax.fori_loop(1, 8, one, 0)

    def z_size(n):
        return z_buf.at[pl.ds(0, 7), z_rows(n)]

    def gather_send(n):
        whole_wait(z_size(n), sum_sem.at[n, 5])
        total = z_buf[0, z_rows(n), :].astype(F32)
        for g in range(1, 8):
            total = total + z_buf[g, z_rows(n), :].astype(F32)
        sums_ref[core, piece(n, place), :] = total.astype(BF)
        mine = sums_ref.at[core, piece(n, place)]

        def one(d, carry):
            send(
                mine,
                mine,
                sum_sem.at[n, 6],
                sum_sem.at[n, 7],
                plane_peer(lax.rem(place + d, 16)),
            )
            return carry

        lax.fori_loop(1, 16, one, 0)

    def last_send(n):
        whole_wait(plane_buf.at[plane_slots(n, 15)], sum_sem.at[n, 7])
        half_sums = sums_ref.at[core, part_rows(n)]
        return send(half_sums, half_sums, sum_sem.at[n, 8], sum_sem.at[n, 9], (a, other_core))

    wait_back(1, back_own, sem.at[11])

    def cycle_rows(which, i):
        return jnp.concatenate(
            [cycle_wide[which, pl.ds(which * 8 + h * 4 + i, 32, stride=16), :] for h in range(2)], axis=1
        )

    for i in (0, 3, 1, 2):
        near_cycles[i + 1] = (cycle_rows(1, i) * cycle_weight_ref[i]).astype(BF)
    near_copies = [
        send(near_cycles.at[1], near_cycles.at[5], near_sem.at[0], near_sem.at[1], (north, b)),
        send(near_cycles.at[4], near_cycles.at[0], near_sem.at[2], near_sem.at[3], (south, b)),
    ]

    def make_grad(r):
        spatial = jnp.dot(wide_ref[0], near_cycles[r], preferred_element_type=F32).astype(BF)
        return (cot_wide[r].astype(F32) + spatial.astype(F32)).astype(BF)

    whole_wait(side_size(cot_wide), sem.at[6])
    whole_wait(lat_size(cot_wide), sem.at[30])
    for i in range(4):
        grad = make_grad(i + 1)
        grad_wide[i + 1] = grad
        grad_own[i * WIDTH : i * WIDTH + WIDTH, :] = grad[16 : 16 + WIDTH]
    def filter_terms(k):
        own = slice(k * 256, k * 256 + 256)
        term = jnp.dot(filtered_t[own, :], grad_own[...], preferred_element_type=F32)
        for h in range(2):
            terms[h, own, :] = term[:, h * 128 : h * 128 + 128]

    filter_terms(0)
    filter_terms(1)
    first_copy = core_send(1)
    filter_terms(2)
    filter_terms(3)
    second_copy = core_send(2)
    plane_send(1, first_copy)
    fore_own = own_order(0, sem.at[38], sem.at[39], sem.at[40], sem.at[41])

    degrees = pl.ds(pl.multiple_of((y_lo * 4 + b) * 48, 16), 48)
    term = lax.dot_general(
        spec[degrees, 0:256],
        scaled_s[degrees, :],
        (((0,), (0,)), ((), ())),
        preferred_element_type=F32,
    )
    for h in range(2):
        terms[h, 1024:1280, :] = term[:, h * 128 : h * 128 + 128]

    spectral_copy = core_send(0)
    plane_send(2, second_copy)

    def finish_output(i):
        fore = cycle_rows(0, i).astype(BF)
        spatial = jnp.dot(wide_ref[1, 16 : 16 + WIDTH, :], fore, preferred_element_type=F32)
        out_ref[i] = (hidden[i].astype(F32) + spatial.astype(BF).astype(F32)).astype(BF)

    for copy in near_copies:
        copy.wait()
    for r in (0, 5):
        grad_wide[r] = make_grad(r)

    def field_grad(i):
        total = grad_own[i * WIDTH : i * WIDTH + WIDTH, :].astype(F32)
        done = []
        for block in range(2):
            sums = stencil(grad_wide, band_back, i, block)
            part = total[block * 96 : block * 96 + 96]
            for k in range(BASIS_COUNT):
                part = part + lax.dot_general(
                    sums[k * 96 : k * 96 + 96],
                    filter_ref[k * 256 : k * 256 + 256, :],
                    (((1,), (1,)), ((), ())),
                    preferred_element_type=F32,
                )
            done.append(part)
        grad_ref[i] = jnp.concatenate(done).astype(BF)

    z_send(1)
    field_grad(0)
    plane_send(0, spectral_copy)
    z_send(2)
    field_grad(1)
    gather_send(1)
    z_send(0)
    field_grad(2)
    gather_send(2)
    field_grad(3)
    gather_send(0)
    last_copies = [last_send(1)]
    wait_back(0, fore_own, sem.at[40])
    for i in range(4):
        finish_output(i)
    last_copies.append(last_send(2))
    last_copies.append(last_send(0))

    whole_wait(side_size(field_wide), sem.at[0])
    whole_wait(lat_size(field_wide), sem.at[24])
    whole_wait(side_size(cot_wide), sem.at[5])
    whole_wait(lat_size(cot_wide), sem.at[29])
    wait_partial(1, sem.at[26], None)
    wait_partial(0, sem.at[7], None)
    whole_wait(table_buf.at[:, 0, 0, 0], sem.at[2])
    whole_wait(table_buf.at[pl.ds(0, 6), 0], sem.at[31])
    whole_wait(mode_buf.at[0, pl.ds(0, 7)], sem.at[36])
    whole_wait(mode_buf.at[0, pl.ds(0, 7)], sem.at[37])
    whole_wait(cycle_buf.at[0, pl.ds(0, 16 * 31), :], sem.at[10])
    whole_wait(cycle_buf.at[0, pl.ds(0, 16 * 31), :], sem.at[39])
    for n in range(3):
        whole_wait(plane_buf.at[plane_slots(n, 15)], sum_sem.at[n, 2])
        whole_wait(z_size(n), sum_sem.at[n, 4])
        whole_wait(plane_buf.at[plane_slots(n, 15)], sum_sem.at[n, 6])
    for copy in last_copies:
        copy.wait()


def finish_kernel(sums_hbm, out_hbm, grad_hbm, out_ref, grad_ref, filter_ref, spectral_ref, *scratch):
    sums_ref, filter_vmem, spectral_vmem, out_vmem, grad_vmem, sem = scratch
    b = lax.axis_index("lon")
    copies = [
        pltpu.make_async_copy(sums_hbm, sums_ref, sem.at[0]),
        pltpu.make_async_copy(out_hbm, out_vmem, sem.at[1]),
        pltpu.make_async_copy(grad_hbm, grad_vmem, sem.at[2]),
    ]
    for copy in copies:
        copy.start()
    copies[0].wait()
    grid_scale = (LATITUDES * LONGITUDES) ** (-0.5)
    for k in range(BASIS_COUNT):
        for h in range(2):
            rows, lanes = slice(k * 256, k * 256 + 256), slice(h * 128, h * 128 + 128)
            filter_vmem[rows, lanes] = sums_ref[h, rows, :].astype(F32) * grid_scale
        rows = pl.ds(k * 256, 256)
        copies.append(
            pltpu.make_async_copy(filter_vmem.at[rows], filter_ref.at[rows], sem.at[3 + k])
        )
        copies[-1].start()
    columns = sums_ref[lax.div(b, 2), 1024:1280, :].astype(F32)
    columns = columns * (2 * ORDERS * DEGREES) ** (-0.5)
    spectral_vmem[...] = jnp.where(
        lax.rem(b, 2) == 0, columns[:, 0:64], columns[:, 64:128]
    ).T
    copies.append(pltpu.make_async_copy(spectral_vmem, spectral_ref, sem.at[7]))
    copies[-1].start()
    for n, (staged, target) in enumerate(((out_vmem, out_ref), (grad_vmem, grad_ref))):
        copies[1 + n].wait()
        copies.append(pltpu.make_async_copy(staged, target, sem.at[8 + n]))
        copies[-1].start()
    for copy in copies[3:]:
        copy.wait()


def finish_call(sums, out, grad):
    anywhere = pl.BlockSpec(memory_space=pl.ANY)
    return pl.pallas_call(
        finish_kernel,
        out_shape=(
            jax.ShapeDtypeStruct((4, WIDTH, 256), BF),
            jax.ShapeDtypeStruct((4, WIDTH, 256), BF),
            jax.ShapeDtypeStruct((1024, 256), F32),
            jax.ShapeDtypeStruct((64, 256), F32),
        ),
        in_specs=[anywhere] * 3,
        out_specs=(anywhere,) * 4,
        scratch_shapes=[
            pltpu.VMEM((2, ROWS, 128), BF),
            pltpu.VMEM((1024, 256), F32),
            pltpu.VMEM((64, 256), F32),
            pltpu.VMEM((4, WIDTH, 256), BF),
            pltpu.VMEM((4, WIDTH, 256), BF),
            pltpu.SemaphoreType.DMA((10,)),
        ],
        compiler_params=pltpu.CompilerParams(vmem_limit_bytes=60 * 2**20),
        name="finish",
    )(sums, out, grad)


def block_call(cycle_weight, field, cotangent, legendre, gain, mixing, filter_weight, support):
    pick, gain_pick = unpack_constants()
    wide, across = trig_tables()
    vmem = pl.BlockSpec(memory_space=pltpu.VMEM)
    smem = pl.BlockSpec(memory_space=pltpu.SMEM)
    anywhere = pl.BlockSpec(memory_space=pl.ANY)
    dma = pltpu.SemaphoreType.DMA
    return pl.pallas_call(
        block_kernel,
        out_shape=(
            jax.ShapeDtypeStruct((4, WIDTH, 256), BF),
            jax.ShapeDtypeStruct((4, WIDTH, 256), BF),
            jax.ShapeDtypeStruct((2, ROWS, 128), BF),
        ),
        in_specs=[smem, anywhere, anywhere, vmem, vmem] + [anywhere] * 9,
        out_specs=(vmem,) * 3,
        scratch_shapes=[
            pltpu.VMEM((256, 256), BF),
            pltpu.VMEM((1024, 256), BF),
            pltpu.VMEM((3, 128, 256), BF),
            pltpu.VMEM((2, 48, 256), BF),
            pltpu.VMEM((2, WIDE, 32), BF),
            pltpu.VMEM((2, 32, WIDTH), BF),
            pltpu.VMEM((18, LATITUDES), jnp.int32),
            pltpu.VMEM((18, LATITUDES), jnp.int32),
            pltpu.VMEM((18, LATITUDES), F32),
            pltpu.VMEM((6, WIDE, 256), BF),
            pltpu.VMEM((6, WIDE, 256), BF),
            pltpu.VMEM((6, WIDE, 256), BF),
            pltpu.VMEM((4, 384, 384), BF),
            pltpu.VMEM((4, 384, 384), BF),
            pltpu.VMEM((768, 1024), BF),
            pltpu.VMEM((1024, 768), BF),
            pltpu.VMEM((4, WIDTH, 256), BF),
            pltpu.VMEM((768, 256), BF),
            pltpu.VMEM((2, 256, 128), F32),
            pltpu.VMEM((2, 8, LON, 8, 128), F32),
            pltpu.VMEM((16, 128), F32),
            pltpu.VMEM((16, 128), BF),
            pltpu.VMEM((3, 16, 128), BF),
            pltpu.VMEM((16, 32, 128), BF),
            pltpu.VMEM((8, 2, 2, 2, 32, 128), BF),
            pltpu.VMEM((2, 8, 2, 4, 16, 128), BF),
            pltpu.VMEM((8, 2, 64, DEGREES), BF),
            pltpu.VMEM((DEGREES, 1024), BF),
            pltpu.VMEM((DEGREES, 256), F32),
            pltpu.VMEM((DEGREES, 512), BF),
            pltpu.VMEM((DEGREES, 256), BF),
            pltpu.VMEM((DEGREES, 512), BF),
            pltpu.VMEM((2, 512, 128), BF),
            pltpu.VMEM((2, 512, 128), BF),
            pltpu.VMEM((2, 512, 128), F32),
            pltpu.VMEM((6, 32, 256), BF),
            pltpu.VMEM((2, ROWS, 128), F32),
            pltpu.VMEM((ROWS, 128), BF),
            pltpu.VMEM((ROWS, 128), BF),
            pltpu.VMEM((ROWS, 128), BF),
            pltpu.VMEM((15 * PIECE, 128), BF),
            pltpu.VMEM((8, PIECE, 128), BF),
            dma((42,)),
            dma((1, 2, 3)),
            dma((4,)),
            dma((11,)),
            dma((3, 10)),
        ],
        compiler_params=pltpu.CompilerParams(
            collective_id=0, has_side_effects=True, vmem_limit_bytes=60 * 2**20
        ),
        name="block",
    )(
        cycle_weight,
        field,
        cotangent,
        legendre,
        gain,
        mixing,
        filter_weight,
        jnp.asarray(pick, BF),
        jnp.asarray(gain_pick, BF),
        jnp.asarray(wide, BF),
        jnp.asarray(across, BF),
        *support,
    )


def per_device(
    field,
    cotangent,
    legendre,
    cycle_weight,
    support_tap,
    support_basis,
    support_weight,
    filter_weight,
    spectral_weight,
    spectral_gain,
):
    table = legendre.reshape(16, 3, 128, 4).transpose(0, 1, 3, 2).reshape(16, 12, 128)
    table = jnp.pad(table, ((0, 0), (0, 4), (0, 0)))
    output, grad_field, sums = block_call(
        cycle_weight,
        field,
        cotangent,
        table,
        spectral_gain,
        spectral_weight,
        filter_weight.reshape(1024, 256),
        (support_tap.T, support_basis.T, support_weight.T),
    )
    output, grad_field, grad_filter, grad_spectral = finish_call(sums, output, grad_field)
    return (output, grad_field, grad_filter.reshape(4, 256, 256), grad_spectral.T)


def solution(mesh):
    placed = (
        P("lat", "lon", None),
        P("lat", "lon", None),
        P(None, None, "lat"),
        P("lat"),
        P(),
        P(),
        P(),
        P(),
        P(),
        P("lat", "lon"),
    )
    return jax.shard_map(
        per_device,
        mesh=mesh,
        in_specs=placed,
        out_specs=(P("lat", "lon", None), P("lat", "lon", None), P(), P(None, "lon")),
        check_vma=False,
    )
```
